1024 devices in a mesh: blk: 128 (over y_lo, z, core), grp: 8 (over x, y_hi).
Axes of the slice: x: 4, y: 8 (y_hi: 2, y_lo: 4; y = y_hi * 4 + y_lo), z: 16, core: 2. Of those that a mesh axis runs over, the one named last changes fastest.
Arguments:
- embeddings: bfloat16 [196608, 1280], P(('blk', 'grp')), may hold values from -48 to 48
- proj_weight: bfloat16 [1280, 1024], replicated, may hold values from -0.15625 to 0.15625
- labels: int32 [196608], replicated, may hold values from 0 to 3071
- flags: int32 [196608], replicated, may hold values 0 or 1
Outputs:
- row_loss: float32 [196608], P(('blk', 'grp'))
- head_grad: float32 [1280, 1024], P('blk', 'grp')
The draws below stay inside these ranges and needn't reach their ends.
All inputs are finite; a program needn't handle non-finite values.
Results may differ from the reference program's by a relative error of at most 0.0019.
Values may be sent and summed in bfloat16 or wider, within the bound.
A program may use at most 64 MiB of HBM per device.

```python
import jax
import jax.numpy as jnp
from jax import lax

E = 1280
P_SIZE = 1024
ROW_DEV = 192
HALF = 4
ROWS = 196608
PER_BLOCK = 24
CLASSES = 3072
N_BLK = 128
N_GRP = 8


def class_labels(key):
    label_key = jax.random.fold_in(key, 11)
    places = jnp.arange(ROWS, dtype=jnp.int32)
    blocks = places // (ROW_DEV * N_GRP)
    shifts = jax.random.randint(jax.random.fold_in(label_key, 1), (ROWS,), -1, 2, dtype=jnp.int32)
    inner = jax.random.randint(jax.random.fold_in(label_key, 2), (ROWS,), 0, PER_BLOCK, dtype=jnp.int32)
    result = (blocks + shifts) % N_BLK * PER_BLOCK + inner
    result = result.at[0].set(0)
    result = result.at[ROWS - 1].set(CLASSES - 1)
    return result.astype(jnp.int32)


def draw_labels(key, part):
    return class_labels(key)


def draw_embeddings(key, part):
    classes = class_labels(key)
    key = jax.random.fold_in(key, 5)
    protos = jnp.clip(jax.random.normal(jax.random.fold_in(key, 1), (CLASSES, E), jnp.float32), -4.0, 4.0)
    noise = jnp.clip(jax.random.normal(jax.random.fold_in(key, 2), (ROWS, E), jnp.float32), -4.0, 4.0)
    return (protos[classes] + 0.7 * noise).astype(jnp.bfloat16)


def place_ends(entries, stream_key, smallest, largest):
    dims = entries.shape
    spot = [jax.random.randint(jax.random.fold_in(stream_key, axis), (), 0, dims[axis]) for axis in range(len(dims))]
    entries = entries.at[tuple(spot)].set(smallest)
    longest = dims.index(max(dims))
    spot[longest] = (spot[longest] + 1) % dims[longest]
    return entries.at[tuple(spot)].set(largest)


def gaussian(stream_key, extent, spread, bound, held_as=jnp.bfloat16):
    entries = jax.random.normal(stream_key, extent, jnp.float32) * spread
    return jnp.minimum(jnp.maximum(entries, -bound), bound).astype(held_as)


def setup_inputs(seed: int = 0) -> dict:
    streams_of = jax.random.split(jax.random.key(seed), 5)
    return {
        "embeddings": draw_embeddings(jax.random.fold_in(streams_of[4], 71), 0),
        "proj_weight": gaussian(streams_of[1], (E, P_SIZE), E ** -0.5, 0.15625),
        "labels": draw_labels(jax.random.fold_in(streams_of[4], 71), 0),
        "flags": place_ends((jax.random.randint(streams_of[3], (ROWS,), 0, 2) < 1).astype(jnp.int32), jax.random.fold_in(streams_of[3], 1), 0, 1),
    }


SOFTMAX_TEMP = 0.1

def reference(embeddings, proj_weight, labels, flags):
    z = jnp.dot(embeddings, proj_weight, preferred_element_type=jnp.float32)
    norm = jnp.sqrt(lax.optimization_barrier(jnp.sum(z * z, axis=1, keepdims=True)) + 1e-06)
    zn = z / norm
    unit_embeddings = zn.astype(jnp.bfloat16)
    weight = jnp.where(flags == 1, 0.5, 1.0).astype(jnp.float32)
    span = 2 * HALF + 1
    width_c = span * ROW_DEV
    offsets = jnp.arange(-HALF, HALF + 1, dtype=jnp.int32)
    unit_q = unit_embeddings.reshape(N_BLK, N_GRP, ROW_DEV, P_SIZE)
    label_q = labels.reshape(N_BLK, N_GRP, ROW_DEV)
    weight_q = weight.reshape(N_BLK, N_GRP, ROW_DEV)
    place = jnp.arange(width_c, dtype=jnp.int32)
    selfpos = HALF * ROW_DEV + jnp.arange(ROW_DEV, dtype=jnp.int32)
    notself = place[None, :] != selfpos[:, None]

    def block_window(array, index):
        picks = ((index + offsets) % N_BLK).astype(jnp.int32)
        taken = jnp.take(array, picks, axis=0)
        taken = jnp.swapaxes(taken, 0, 1)
        return taken.reshape((N_GRP, width_c) + array.shape[3:])

    def tile(index):
        anchor_rows = unit_q[index]
        column_slice = block_window(unit_q, index)
        similarity_scores = jnp.einsum('lhs,lys->lhy', anchor_rows.astype(jnp.float32), column_slice.astype(jnp.float32)) / SOFTMAX_TEMP
        col_lab = block_window(label_q, index)
        same = jnp.logical_and(label_q[index][:, :, None] == col_lab[:, None, :], notself[None])
        return (similarity_scores, same, column_slice)

    def first_pass(index):
        similarity_scores, same, column_slice = tile(index)
        denom = lax.optimization_barrier(jnp.sum(jnp.where(notself[None], jnp.exp(similarity_scores), 0.0), axis=2))
        possum = lax.optimization_barrier(jnp.sum(jnp.where(same, similarity_scores, 0.0), axis=2))
        count = lax.optimization_barrier(jnp.sum(same.astype(jnp.float32), axis=2))
        return (denom, possum, count)
    denom, possum, count = lax.map(first_pass, jnp.arange(N_BLK, dtype=jnp.int32))
    inv_count = 1.0 / jnp.maximum(count, 1.0)
    row_loss = (weight_q * (jnp.log(denom) - possum * inv_count)).reshape(ROWS)
    recip = 1.0 / denom

    def second_pass(index):
        similarity_scores, same, column_slice = tile(index)
        expo = jnp.where(notself[None], jnp.exp(similarity_scores), 0.0)
        samef = same.astype(jnp.float32)
        row_coefficient = weight_q[index][:, :, None] * (expo * recip[index][:, :, None] - samef * inv_count[index][:, :, None])
        col_w = block_window(weight_q, index)
        col_r = block_window(recip, index)
        col_c = block_window(inv_count, index)
        column_coefficient = col_w[:, None, :] * (expo * col_r[:, None, :] - samef * col_c[:, None, :])
        pair_logits = ((row_coefficient + column_coefficient) / SOFTMAX_TEMP).astype(jnp.bfloat16)
        return jnp.einsum('ohn,onl->ohl', pair_logits.astype(jnp.float32), column_slice.astype(jnp.float32))
    grad_unit = lax.map(second_pass, jnp.arange(N_BLK, dtype=jnp.int32)).reshape(ROWS, P_SIZE)
    grad_z = (grad_unit - zn * lax.optimization_barrier(jnp.sum(zn * grad_unit, axis=1, keepdims=True))) / norm
    grad_zb = grad_z.astype(jnp.bfloat16)
    head_grad = jnp.dot(embeddings.T, grad_zb, preferred_element_type=jnp.float32)
    return (row_loss, head_grad)
```

```python
import functools

import jax
import jax.numpy as jnp
from jax import lax
from jax.experimental import pallas as pl
from jax.experimental.pallas import tpu as pltpu
from jax.sharding import PartitionSpec as P

MESH = pl.DeviceIdType.MESH
F32 = jnp.float32
BF16 = jnp.bfloat16

NX, NYH, NYL, NZ = 4, 2, 4, 16
NY = NYH * NYL
ROWS, E, WIDTH = 192, 1280, 1024
SLOTS = 9
PIECES = 4
PIECE = ROWS // PIECES
HALFROWS = ROWS // 2
SLICE = 128
YROWS = E // NYL // 2
ZROWS = 10
ZPAD = 16
SCALE = 10.0
YTYPE = F32


def kernel(
    emb_hbm, w_hbm, lab_hbm, flag_hbm, loss_ref, head_ref,
    w_v, lab_v, flag_v, lw, embg, zn, win, ex, pr, st, gu, gzs, gzg, part, yb, ysum, zs, zb,
    load_sem, halo_send, halo_recv, x_send, x_recv, st_send, st_recv,
    g_send, g_recv, y_send, y_recv, z_send, z_recv,
):
    blk = lax.axis_index("blk")
    grp = lax.axis_index("grp")
    blocks = 2 * NYL * NZ
    core = lax.rem(blk, 2)
    chip = blk // 2
    z_me = lax.rem(chip, NZ)
    yl_me = chip // NZ
    x_me = grp // NYH
    yh_me = lax.rem(grp, NYH)
    y_me = yh_me * NYL + yl_me
    own_x = x_me * 2 + core

    def wrap(value, size):
        return lax.rem(value + size, size)

    def chip_peer(step, which):
        return wrap(chip + step, blocks // 2) * 2 + which, grp

    def x_peer(step, which):
        return chip * 2 + which, wrap(x_me + step, NX) * NYH + yh_me

    sibling = (chip * 2 + 1 - core, grp)
    z_core = z_me // (NZ // 2)

    def remote(src, dst, send, recv, device):
        return pltpu.make_async_remote_copy(
            src_ref=src, dst_ref=dst, send_sem=send, recv_sem=recv, device_id=device, device_id_type=MESH
        )

    own_rows = pl.ds(pl.multiple_of(own_x * ROWS, 16), ROWS)
    loads = [pltpu.make_async_copy(emb_hbm, embg.at[own_rows, :], load_sem.at[0])]
    for n in range(4):
        columns = pl.ds(n * 256, 256)
        loads.append(pltpu.make_async_copy(w_hbm.at[:, columns], w_v.at[:, columns], load_sem.at[1 + n]))
    loads.append(pltpu.make_async_copy(lab_hbm, lab_v, load_sem.at[5]))
    loads.append(pltpu.make_async_copy(flag_hbm, flag_v, load_sem.at[6]))
    for load in loads:
        load.start()

    barrier = pltpu.get_barrier_semaphore()

    def greet(device):
        pl.semaphore_signal(barrier, inc=1, device_id=device, device_id_type=MESH)

    for step in (1, -1, 2, -2, 3, -3, 4, -4):
        greet((wrap(blk + step, blocks), grp))
    for step in (1, 2, 3):
        for which in (0, 1):
            greet(x_peer(step, which))

    def greet_y(y_src, carry):
        @pl.when(jnp.logical_or(y_src != y_me, core != yh_me))
        def _():
            greet(((lax.rem(y_src, NYL) * NZ + z_me) * 2 + yh_me, x_me * NYH + y_src // NYL))
        return carry

    lax.fori_loop(0, NY, greet_y, 0)

    def greet_z(z_src, carry):
        @pl.when(jnp.logical_or(z_src != z_me, core != z_core))
        def _():
            greet(((yl_me * NZ + z_src) * 2 + z_core, grp))
        return carry

    lax.fori_loop(0, NZ, greet_z, 0)

    loads[0].wait()
    emb = embg[own_rows, :]
    ssq = jnp.zeros((ROWS, 1), F32)
    for n in range(4):
        columns = pl.ds(n * 256, 256)
        loads[1 + n].wait()
        zc = jnp.dot(emb, w_v[:, columns], preferred_element_type=F32)
        zn[:, columns] = zc
        ssq = ssq + jnp.sum(zc * zc, axis=1, keepdims=True)
    rnorm = 1.0 / jnp.sqrt(ssq + 1e-6)
    for n in range(4):
        columns = pl.ds(n * 256, 256)
        zc = zn[:, columns] * rnorm
        zn[:, columns] = zc
        win[4, :, columns] = zc.astype(BF16)

    greeted = (
        8 + 6 + NY + NZ
        - jnp.where(core == yh_me, 1, 0).astype(jnp.int32)
        - jnp.where(core == z_core, 1, 0).astype(jnp.int32)
    )
    pl.semaphore_wait(barrier, greeted)

    ahead, behind = chip_peer(1, core), chip_peer(-1, core)
    sends = []

    def halo(src_slot, dst_slot, p, send, device):
        rows = pl.ds(p * PIECE, PIECE)
        copy = remote(
            win.at[src_slot, rows, :], win.at[dst_slot, rows, :],
            halo_send.at[send, p], halo_recv.at[dst_slot, p], device,
        )
        copy.start()
        sends.append(copy)

    def halo_wait(slot, p):
        rows = pl.ds(p * PIECE, PIECE)
        remote(
            win.at[slot, rows, :], win.at[slot, rows, :],
            halo_send.at[0, p], halo_recv.at[slot, p], sibling,
        ).wait_recv()

    for p in range(PIECES):
        halo(4, 2, p, 0, ahead)
        halo(4, 6, p, 1, behind)
        halo(4, 3 + 2 * core, p, 2, sibling)

    right, left = x_peer(1, core), x_peer(-1, core)

    def slot_rows(x_step, which, half=None):
        start = (wrap(x_me + x_step, NX) * 2 + which) * ROWS
        if half is None:
            return pl.ds(pl.multiple_of(start, 16), ROWS)
        return pl.ds(pl.multiple_of(start + half * HALFROWS, 16), HALFROWS)

    def x_copy(rows, send, recv, half, device):
        copy = remote(embg.at[rows, :], embg.at[rows, :], x_send.at[send], x_recv.at[recv, half], device)
        copy.start()
        sends.append(copy)

    def x_wait(rows, recv, half):
        remote(embg.at[rows, :], embg.at[rows, :], x_send.at[0], x_recv.at[recv, half], sibling).wait_recv()

    x_copy(own_rows, 0, 0, 0, sibling)
    x_copy(own_rows, 1, 1, 0, right)
    x_copy(own_rows, 2, 2, 0, left)

    loads[5].wait()
    loads[6].wait()
    odd = lax.rem(grp, 2) == 1

    def label_row(ref, block):
        row = block * 12 + (3 * grp) // 2
        return ref[pl.ds(row, 1), :].astype(F32), ref[pl.ds(row + 1, 1), :].astype(F32)

    lw[...] = jnp.zeros_like(lw)
    for slot in range(SLOTS):
        low, high = label_row(lab_v, wrap(blk + slot - 4, blocks))
        lw[slot : slot + 1, 0:128] = low
        lw[slot : slot + 1, 128:256] = high
    low, high = label_row(flag_v, blk)
    lw[SLOTS : SLOTS + 1, 0:128] = low
    lw[SLOTS : SLOTS + 1, 128:256] = high
    plain = lw[...]
    lw[...] = jnp.where(odd, pltpu.roll(plain, 192, 1), plain)
    turned = jnp.transpose(jnp.concatenate([lw[...], jnp.zeros((112, 256), F32)], axis=0))
    own_lab = turned[:ROWS, 4:5]
    own_w = jnp.where(turned[:ROWS, SLOTS : SLOTS + 1] == 1.0, 0.5, 1.0)
    diagonal = lax.broadcasted_iota(jnp.int32, (ROWS, ROWS), 0) == lax.broadcasted_iota(
        jnp.int32, (ROWS, ROWS), 1
    )

    def same_label(slot, own):
        same = own_lab == lw[pl.ds(slot, 1), :ROWS]
        return jnp.logical_and(same, jnp.logical_not(diagonal)) if own else same

    own_unit = win[4]

    def scores(slot, sums, own=False):
        denom, possum, count = sums
        s = SCALE * lax.dot_general(
            own_unit, win[slot], (((1,), (1,)), ((), ())), preferred_element_type=F32
        )
        e = jnp.exp(s)
        if own:
            e = jnp.where(diagonal, 0.0, e)
        same = same_label(slot, own)
        ex[slot] = e
        denom = denom + jnp.sum(e, axis=1, keepdims=True)
        possum = possum + jnp.sum(jnp.where(same, s, 0.0), axis=1, keepdims=True)
        count = count + jnp.sum(jnp.where(same, 1.0, 0.0), axis=1, keepdims=True)
        return denom, possum, count

    nought = jnp.zeros((ROWS, 1), F32)
    sums = scores(4, (nought, nought, nought), own=True)

    for p in range(PIECES):
        halo_wait(2, p)
        halo(2, 0, p, 3, ahead)
        halo(2, 1 + 2 * core, p, 4, sibling)
        halo_wait(6, p)
        halo(6, 8, p, 5, behind)
        halo(6, 5 + 2 * core, p, 6, sibling)
    sums = scores(2, sums)
    sums = scores(6, sums)
    for slot in (5 - 2 * core, 3 - 2 * core, 7 - 2 * core):
        for p in range(PIECES):
            halo_wait(slot, p)
        sums = scores(slot, sums)

    x_wait(slot_rows(-1, core), 1, 0)
    x_copy(slot_rows(-1, core, 0), 3, 3, 0, right)
    x_copy(slot_rows(-1, core), 5, 4, 0, sibling)
    x_wait(slot_rows(1, core), 2, 0)
    x_copy(slot_rows(1, core, 1), 4, 3, 1, left)
    x_copy(slot_rows(1, core), 6, 5, 0, sibling)

    for p in range(PIECES):
        halo_wait(8 - 8 * core, p)
        halo(8 - 8 * core, 7 - 6 * core, p, 7, sibling)
    sums = scores(8 - 8 * core, sums)
    for slot in (8 * core, 1 + 6 * core):
        for p in range(PIECES):
            halo_wait(slot, p)
        sums = scores(slot, sums)

    denom, possum, count = sums
    inv_count = 1.0 / jnp.maximum(count, 1.0)
    own_loss = own_w * (jnp.log(denom) - possum * inv_count)
    own_a = (SCALE * own_w) / denom
    own_c = (SCALE * own_w) * inv_count
    lane = lax.broadcasted_iota(jnp.int32, (ROWS, 128), 1)
    columns = jnp.where(lane == 0, own_a, jnp.where(lane == 1, own_c, own_loss))
    flat = jnp.transpose(jnp.concatenate([columns, jnp.zeros((64, 128), F32)], axis=0))
    st[4] = flat[:8]
    loss_ref[...] = flat[2:3]
    steps = (4, -4, 3, -3, 2, -2, 1, -1)
    for i, step in enumerate(steps):
        copy = remote(
            st.at[4], st.at[4 - step], st_send.at[i], st_recv.at[4 - step], (wrap(blk + step, blocks), grp)
        )
        copy.start()
        sends.append(copy)

    for half in (0, 1):
        x_wait(slot_rows(2, core, half), 3, half)
        x_copy(slot_rows(2, core, half), 7 + half, 6, half, sibling)

    def pairs(slot, own=False):
        row = st[slot]
        same = same_label(slot, own)
        value = ex[slot] * (own_a + row[0:1, :ROWS]) - jnp.where(same, own_c + row[1:2, :ROWS], 0.0)
        pr[slot] = value.astype(BF16)

    pairs(4, own=True)
    for step in (1, -1, 2, -2, 3, -3, 4, -4):
        slot = 4 + step
        remote(st.at[slot], st.at[slot], st_send.at[0], st_recv.at[slot], sibling).wait_recv()
        pairs(slot)

    along = jnp.zeros((ROWS, 1), F32)
    for n in range(4):
        columns = pl.ds(n * 256, 256)
        total = jnp.dot(pr[0], win[0, :, columns], preferred_element_type=F32)
        for slot in range(1, SLOTS):
            total = total + jnp.dot(pr[slot], win[slot, :, columns], preferred_element_type=F32)
        gu[:, columns] = total
        along = along + jnp.sum(zn[:, columns] * total, axis=1, keepdims=True)
    for j in range(2 * NX):
        columns = pl.ds(j * SLICE, SLICE)
        gzs[j] = ((gu[:, columns] - zn[:, columns] * along) * rnorm).astype(BF16)
    g_sends = []
    for step in (2, 1, 3, 0):
        for which in (0, 1):
            if step == 0 and which == 0:
                target, device = x_me * 2 + 1 - core, sibling
            elif step == 0:
                continue
            else:
                target, device = wrap(x_me + step, NX) * 2 + which, x_peer(step, which)
            copy = remote(
                gzs.at[target], gzg.at[own_rows, :], g_send.at[2 * step + which], g_recv.at[own_x], device
            )
            copy.start()
            sends.append(copy)
    gzg[own_rows, :] = gzs[own_x]

    x_wait(slot_rows(0, 1 - core), 0, 0)
    x_wait(slot_rows(-1, 1 - core), 4, 0)
    x_wait(slot_rows(1, 1 - core), 5, 0)
    for half in (0, 1):
        x_wait(slot_rows(2, 1 - core, half), 6, half)
    for step, which in ((0, 1 - core), (1, 0), (1, 1), (3, 0), (3, 1), (2, 0), (2, 1)):
        source = wrap(x_me + step, NX) * 2 + which
        rows = slot_rows(step, which)
        remote(gzs.at[0], gzg.at[rows, :], g_send.at[0], g_recv.at[source], sibling).wait_recv()

    for n in range(E // 256):
        columns = pl.ds(n * 256, 256)
        piece = lax.dot_general(
            gzg[...], embg[:, columns], (((0,), (0,)), ((), ())), preferred_element_type=F32
        )
        part[pl.ds(n * 256, 256), :] = jnp.transpose(piece).astype(YTYPE)

    def y_rows(yl, which):
        return pl.ds(yl * (2 * YROWS) + which * YROWS, YROWS)

    def y_self(yl, which):
        return jnp.logical_and(core == yh_me, jnp.logical_and(yl_me == yl, core == which))

    def y_copy(yl, which):
        return remote(
            part.at[y_rows(yl, which), :], yb.at[y_me], y_send.at[yl, which], y_recv.at[y_me],
            ((yl * NZ + z_me) * 2 + which, x_me * NYH + core),
        )

    for yl in range(NYL):
        for which in (0, 1):
            @pl.when(jnp.logical_not(y_self(yl, which)))
            def _(yl=yl, which=which):
                y_copy(yl, which).start()

            @pl.when(y_self(yl, which))
            def _(yl=yl, which=which):
                yb[y_me] = part[y_rows(yl, which), :]

    for src in range(NY):
        @pl.when(jnp.logical_or(y_me != src, core != yh_me))
        def _(src=src):
            remote(yb.at[src], yb.at[src], y_send.at[0, 0], y_recv.at[src], sibling).wait_recv()

    total = yb[0].astype(F32)
    for src in range(1, NY):
        total = total + yb[src].astype(F32)
    ysum[0:YROWS, :] = total
    ysum[YROWS:, :] = jnp.zeros((ZPAD, SLICE), F32)

    for i in range(NZ):
        zs[i] = ysum[i * ZROWS : i * ZROWS + ZPAD, :]

    def z_copy(i, which):
        return remote(
            zs.at[i * 2 + which], zb.at[z_me], z_send.at[i, which], z_recv.at[z_me],
            ((yl_me * NZ + core * (NZ // 2) + i) * 2 + which, grp),
        )

    def z_self(i, which):
        return jnp.logical_and(z_me == core * (NZ // 2) + i, core == which)

    for i in range(NZ // 2):
        for which in (0, 1):
            @pl.when(jnp.logical_not(z_self(i, which)))
            def _(i=i, which=which):
                z_copy(i, which).start()

            @pl.when(z_self(i, which))
            def _(i=i, which=which):
                zb[z_me] = zs[i * 2 + which]

    for src in range(NZ):
        @pl.when(jnp.logical_or(z_me != src, core != z_core))
        def _(src=src):
            remote(zb.at[src], zb.at[src], z_send.at[0, 0], z_recv.at[src], sibling).wait_recv()

    total = zb[0]
    for src in range(1, NZ):
        total = total + zb[src]
    head_ref[...] = total[:ZROWS, :]

    for copy in sends:
        copy.wait_send()
    for yl in range(NYL):
        for which in (0, 1):
            @pl.when(jnp.logical_not(y_self(yl, which)))
            def _(yl=yl, which=which):
                y_copy(yl, which).wait_send()
    for i in range(NZ // 2):
        for which in (0, 1):
            @pl.when(jnp.logical_not(z_self(i, which)))
            def _(i=i, which=which):
                z_copy(i, which).wait_send()


def on_device(embeddings, proj_weight, labels, flags):
    dma = pltpu.SemaphoreType.DMA
    loss, head = pl.pallas_call(
        kernel,
        out_shape=(
            jax.ShapeDtypeStruct((1, 256), F32),
            jax.ShapeDtypeStruct((ZROWS, SLICE), F32),
        ),
        in_specs=[pl.BlockSpec(memory_space=pl.ANY)] * 4,
        out_specs=(
            pl.BlockSpec(memory_space=pltpu.VMEM),
            pl.BlockSpec(memory_space=pltpu.VMEM),
        ),
        scratch_shapes=[
            pltpu.VMEM((E, WIDTH), BF16),
            pltpu.VMEM((1536, 128), jnp.int32),
            pltpu.VMEM((1536, 128), jnp.int32),
            pltpu.VMEM((16, 256), F32),
            pltpu.VMEM((2 * NX * ROWS, E), BF16),
            pltpu.VMEM((ROWS, WIDTH), F32),
            pltpu.VMEM((SLOTS, ROWS, WIDTH), BF16),
            pltpu.VMEM((SLOTS, ROWS, ROWS), F32),
            pltpu.VMEM((SLOTS, ROWS, ROWS), BF16),
            pltpu.VMEM((SLOTS, 8, 256), F32),
            pltpu.VMEM((ROWS, WIDTH), F32),
            pltpu.VMEM((2 * NX, ROWS, SLICE), BF16),
            pltpu.VMEM((2 * NX * ROWS, SLICE), BF16),
            pltpu.VMEM((E, SLICE), YTYPE),
            pltpu.VMEM((NY, YROWS, SLICE), YTYPE),
            pltpu.VMEM((YROWS + ZPAD, SLICE), F32),
            pltpu.VMEM((NZ, ZPAD, SLICE), F32),
            pltpu.VMEM((NZ, ZPAD, SLICE), F32),
            dma((7,)),
            dma((8, PIECES)),
            dma((SLOTS, PIECES)),
            dma((9,)),
            dma((7, 2)),
            dma((8,)),
            dma((SLOTS,)),
            dma((8,)),
            dma((2 * NX,)),
            dma((NYL, 2)),
            dma((NY,)),
            dma((NZ // 2, 2)),
            dma((NZ,)),
        ],
        compiler_params=pltpu.CompilerParams(
            collective_id=0, has_side_effects=True, vmem_limit_bytes=60 * 2**20
        ),
        name="contrastive_loss_and_head_gradient",
    )(embeddings, proj_weight, labels.reshape(1536, 128), flags.reshape(1536, 128))
    return loss[0, :ROWS], head


def solution(mesh):
    return jax.shard_map(
        on_device,
        mesh=mesh,
        in_specs=(P(("blk", "grp"), None), P(), P(), P()),
        out_specs=(P(("blk", "grp")), P("blk", "grp")),
        check_vma=False,
    )
```

```python
import functools

import jax
import jax.numpy as jnp
from jax import lax
from jax.experimental import pallas as pl
from jax.experimental.pallas import tpu as pltpu
from jax.sharding import PartitionSpec as P

MESH = pl.DeviceIdType.MESH
F32 = jnp.float32
BF16 = jnp.bfloat16

NX, NYH, NYL, NZ = 4, 2, 4, 16
NY = NYH * NYL
ROWS, E, WIDTH = 192, 1280, 1024
SLOTS = 9
PIECES = 4
PIECE = ROWS // PIECES
HALFROWS = ROWS // 2
SLICE = 128
YROWS = E // NYL // 2
YPART = YROWS // 2
ZROWS = 10
SCALE = 10.0
YTYPE = BF16


def kernel(
    emb_hbm, w_hbm, lab_hbm, flag_hbm, loss_ref, head_ref,
    w_v, lab_v, flag_v, lw, embg, zn, win, ex, sc, pr, st, tp, tpr, gu, gzs, gzg, part, yb, ysum, zs, zb,
    load_sem, halo_send, halo_recv, x_send, x_recv, st_send, st_recv, tp_send, tp_recv,
    g_send, g_recv, y_send, y_recv, z_send, z_recv,
):
    blk = lax.axis_index("blk")
    grp = lax.axis_index("grp")
    blocks = 2 * NYL * NZ
    core = lax.rem(blk, 2)
    chip = blk // 2
    z_me = lax.rem(chip, NZ)
    yl_me = chip // NZ
    x_me = grp // NYH
    yh_me = lax.rem(grp, NYH)
    y_me = yh_me * NYL + yl_me
    own_x = x_me * 2 + core

    def wrap(value, size):
        return lax.rem(value + size, size)

    def chip_peer(step, which):
        return wrap(chip + step, blocks // 2) * 2 + which, grp

    def x_peer(step, which):
        return chip * 2 + which, wrap(x_me + step, NX) * NYH + yh_me

    sibling = (chip * 2 + 1 - core, grp)
    z_core = z_me // (NZ // 2)

    def remote(src, dst, send, recv, device):
        return pltpu.make_async_remote_copy(
            src_ref=src, dst_ref=dst, send_sem=send, recv_sem=recv, device_id=device, device_id_type=MESH
        )

    own_rows = pl.ds(pl.multiple_of(own_x * ROWS, 16), ROWS)
    loads = [pltpu.make_async_copy(emb_hbm, embg.at[own_rows, :], load_sem.at[0])]
    for n in range(4):
        columns = pl.ds(n * 256, 256)
        loads.append(pltpu.make_async_copy(w_hbm.at[:, columns], w_v.at[:, columns], load_sem.at[1 + n]))
    loads.append(pltpu.make_async_copy(lab_hbm, lab_v, load_sem.at[5]))
    loads.append(pltpu.make_async_copy(flag_hbm, flag_v, load_sem.at[6]))
    for load in loads:
        load.start()

    barrier = pltpu.get_barrier_semaphore()

    def greet(device):
        pl.semaphore_signal(barrier, inc=1, device_id=device, device_id_type=MESH)

    for step in (1, -1, 2, -2, 3, -3, 4, -4):
        greet((wrap(blk + step, blocks), grp))
    for step in (1, 2, 3):
        for which in (0, 1):
            greet(x_peer(step, which))

    def greet_y(y_src, carry):
        @pl.when(jnp.logical_or(y_src != y_me, core != yh_me))
        def _():
            greet(((lax.rem(y_src, NYL) * NZ + z_me) * 2 + yh_me, x_me * NYH + y_src // NYL))
        return carry

    lax.fori_loop(0, NY, greet_y, 0)

    def greet_z(z_src, carry):
        @pl.when(jnp.logical_or(z_src != z_me, core != z_core))
        def _():
            greet(((yl_me * NZ + z_src) * 2 + z_core, grp))
        return carry

    lax.fori_loop(0, NZ, greet_z, 0)

    loads[0].wait()
    greeted = (
        8 + 6 + NY + NZ
        - jnp.where(core == yh_me, 1, 0).astype(jnp.int32)
        - jnp.where(core == z_core, 1, 0).astype(jnp.int32)
    )
    ahead, behind = chip_peer(1, core), chip_peer(-1, core)
    sends = []

    def halo(src_slot, dst_slot, p, send, device):
        rows = pl.ds(p * PIECE, PIECE)
        copy = remote(
            win.at[src_slot, rows, :], win.at[dst_slot, rows, :],
            halo_send.at[send, p], halo_recv.at[dst_slot, p], device,
        )
        copy.start()
        sends.append(copy)

    def halo_wait(slot, p):
        rows = pl.ds(p * PIECE, PIECE)
        remote(
            win.at[slot, rows, :], win.at[slot, rows, :],
            halo_send.at[0, p], halo_recv.at[slot, p], sibling,
        ).wait_recv()

    rnorms = []
    for half in (0, 1):
        rows = slice(half * HALFROWS, (half + 1) * HALFROWS)
        emb = embg[pl.ds(pl.multiple_of(own_x * ROWS + half * HALFROWS, 16), HALFROWS), :]
        ssq = jnp.zeros((HALFROWS, 1), F32)
        for n in range(4):
            columns = pl.ds(n * 256, 256)
            if half == 0:
                loads[1 + n].wait()
            zc = jnp.dot(emb, w_v[:, columns], preferred_element_type=F32)
            zn[rows, columns] = zc
            ssq = ssq + jnp.sum(zc * zc, axis=1, keepdims=True)
        rnorms.append(1.0 / jnp.sqrt(ssq + 1e-6))
        for n in range(4):
            columns = pl.ds(n * 256, 256)
            zc = zn[rows, columns] * rnorms[half]
            zn[rows, columns] = zc
            win[4, rows, columns] = zc.astype(BF16)
        if half == 0:
            pl.semaphore_wait(barrier, greeted)
        for p in range(half * (PIECES // 2), (half + 1) * (PIECES // 2)):
            halo(4, 2, p, 0, ahead)
            halo(4, 6, p, 1, behind)
            halo(4, 3 + 2 * core, p, 2, sibling)
    rnorm = jnp.concatenate(rnorms, axis=0)

    right, left = x_peer(1, core), x_peer(-1, core)

    def slot_rows(x_step, which, half=None):
        start = (wrap(x_me + x_step, NX) * 2 + which) * ROWS
        if half is None:
            return pl.ds(pl.multiple_of(start, 16), ROWS)
        return pl.ds(pl.multiple_of(start + half * HALFROWS, 16), HALFROWS)

    def x_copy(rows, send, recv, half, device):
        copy = remote(embg.at[rows, :], embg.at[rows, :], x_send.at[send], x_recv.at[recv, half], device)
        copy.start()
        sends.append(copy)

    def x_wait(rows, recv, half):
        remote(embg.at[rows, :], embg.at[rows, :], x_send.at[0], x_recv.at[recv, half], sibling).wait_recv()

    x_copy(own_rows, 0, 0, 0, sibling)
    for i, half in enumerate((0, 1)):
        x_copy(slot_rows(0, core, half), 1 + i, 1, half, right)
    for i, half in enumerate((1, 0)):
        x_copy(slot_rows(0, core, half), 3 + i, 2, half, left)

    loads[5].wait()
    loads[6].wait()
    odd = lax.rem(grp, 2) == 1

    def label_row(ref, block):
        row = block * 12 + (3 * grp) // 2
        return ref[pl.ds(row, 1), :].astype(F32), ref[pl.ds(row + 1, 1), :].astype(F32)

    lw[...] = jnp.zeros_like(lw)
    for slot in range(SLOTS):
        low, high = label_row(lab_v, wrap(blk + slot - 4, blocks))
        lw[slot : slot + 1, 0:128] = low
        lw[slot : slot + 1, 128:256] = high
    low, high = label_row(flag_v, blk)
    lw[SLOTS : SLOTS + 1, 0:128] = low
    lw[SLOTS : SLOTS + 1, 128:256] = high
    plain = lw[...]
    lw[...] = jnp.where(odd, pltpu.roll(plain, 192, 1), plain)
    turned = jnp.transpose(jnp.concatenate([lw[...], jnp.zeros((112, 256), F32)], axis=0))
    own_lab = turned[:ROWS, 4:5]
    own_w = jnp.where(turned[:ROWS, SLOTS : SLOTS + 1] == 1.0, 0.5, 1.0)
    diagonal = lax.broadcasted_iota(jnp.int32, (ROWS, ROWS), 0) == lax.broadcasted_iota(
        jnp.int32, (ROWS, ROWS), 1
    )

    def same_label(slot, own):
        same = own_lab == lw[pl.ds(slot, 1), :ROWS]
        return jnp.logical_and(same, jnp.logical_not(diagonal)) if own else same

    own_unit = win[4]

    def tile(slot, own=False):
        s = SCALE * lax.dot_general(
            own_unit, win[slot], (((1,), (1,)), ((), ())), preferred_element_type=F32
        )
        e = jnp.exp(s)
        return s, jnp.where(diagonal, 0.0, e) if own else e

    def scores(slot, sums, own=False):
        denom, possum, count = sums
        s, e = tile(slot, own)
        same = same_label(slot, own)
        ex[slot] = e
        sc[slot] = s
        denom = denom + jnp.sum(e, axis=1, keepdims=True)
        possum = possum + jnp.sum(jnp.where(same, s, 0.0), axis=1, keepdims=True)
        count = count + jnp.sum(jnp.where(same, 1.0, 0.0), axis=1, keepdims=True)
        return denom, possum, count

    def cross(rows_slots, slot):
        found = None
        for rows_slot in rows_slots:
            s = SCALE * lax.dot_general(
                win[rows_slot], win[slot], (((1,), (1,)), ((), ())), preferred_element_type=F32
            )
            same = turned[:ROWS, rows_slot : rows_slot + 1] == lw[slot : slot + 1, :ROWS]
            sums = [
                jnp.sum(value, axis=0, keepdims=True)
                for value in (jnp.exp(s), jnp.where(same, s, 0.0), jnp.where(same, 1.0, 0.0))
            ]
            found = sums if found is None else [a + b for a, b in zip(found, sums)]
        return found

    nought = jnp.zeros((ROWS, 1), F32)
    sums = scores(4, (nought, nought, nought), own=True)
    tp[...] = jnp.zeros_like(tp)

    for p in range(PIECES):
        halo_wait(2, p)
        halo(2, 0, p, 3, ahead)
        halo(2, 1 + 2 * core, p, 4, sibling)
        halo_wait(6, p)
        halo(6, 8, p, 5, behind)
        halo(6, 5 + 2 * core, p, 6, sibling)
    x_wait(slot_rows(-1, core, 0), 1, 0)
    x_copy(slot_rows(-1, core, 0), 5, 3, 0, right)
    x_wait(slot_rows(1, core, 1), 2, 1)
    x_copy(slot_rows(1, core, 1), 6, 3, 1, left)
    for slot in (5 - 2 * core, 3 - 2 * core, 7 - 2 * core):
        for p in range(PIECES):
            halo_wait(slot, p)

    for i, (rows_slots, slot, step) in enumerate((((2, 3), 6, 2), ((6,), 2, -2), ((6,), 3, -1))):
        for r, value in enumerate(cross(rows_slots, slot)):
            tp[i, r : r + 1, :ROWS] = value
        copy = remote(
            tp.at[i], tpr.at[i], tp_send.at[i], tp_recv.at[i], (wrap(blk + step, blocks), grp)
        )
        copy.start()
        sends.append(copy)
    for slot in (2, 6, 3, 5):
        sums = scores(slot, sums)
    near = (2, 6, 3, 5, 7 - 6 * core)
    s, e = tile(near[4])
    ex[near[4]] = e
    sc[near[4]] = s
    for i in range(3):
        remote(tpr.at[i], tpr.at[i], tp_send.at[0], tp_recv.at[i], sibling).wait_recv()
    apart = jnp.transpose(jnp.concatenate([tpr[0] + tpr[1] + tpr[2], jnp.zeros((120, 256), F32)], axis=0))
    sums = [value + apart[:ROWS, r : r + 1] for r, value in enumerate(sums)]

    denom, possum, count = sums
    inv_count = 1.0 / jnp.maximum(count, 1.0)
    own_loss = own_w * (jnp.log(denom) - possum * inv_count)
    own_a = (SCALE * own_w) / denom
    own_c = (SCALE * own_w) * inv_count
    lane = lax.broadcasted_iota(jnp.int32, (ROWS, 128), 1)
    columns = jnp.where(lane == 0, own_a, jnp.where(lane == 1, own_c, own_loss))
    flat = jnp.transpose(jnp.concatenate([columns, jnp.zeros((64, 128), F32)], axis=0))
    st[4] = flat[:8]
    loss_ref[...] = flat[2, :ROWS]
    steps = (4, -4, 3, -3, 2, -2, 1, -1)
    for i, step in enumerate(steps):
        copy = remote(
            st.at[4], st.at[4 - step], st_send.at[i], st_recv.at[4 - step], (wrap(blk + step, blocks), grp)
        )
        copy.start()
        sends.append(copy)

    def pass_far(p):
        halo_wait(8 - 8 * core, p)
        halo(8 - 8 * core, 7 - 6 * core, p, 7, sibling)

    pass_far(0)
    pass_far(1)
    x_wait(slot_rows(-1, core, 1), 1, 1)
    x_copy(slot_rows(-1, core), 7, 4, 0, sibling)
    x_wait(slot_rows(1, core, 0), 2, 0)
    x_copy(slot_rows(1, core), 8, 5, 0, sibling)

    def pairs(slot, s, e, own=False):
        if not own:
            remote(st.at[slot], st.at[slot], st_send.at[0], st_recv.at[slot], sibling).wait_recv()
        row = st[slot]
        same = same_label(slot, own)
        value = e * (own_a + row[0:1, :ROWS]) - jnp.where(same, own_c + row[1:2, :ROWS], 0.0)
        held = value.astype(BF16)
        pr[slot] = held
        return jnp.sum(held.astype(F32) * s, axis=1, keepdims=True)

    along = pairs(4, sc[4], ex[4], own=True)
    for slot in near:
        along = along + pairs(slot, sc[slot], ex[slot])
    for n in range(4):
        columns = pl.ds(n * 256, 256)
        total = jnp.dot(pr[4], win[4, :, columns], preferred_element_type=F32)
        for slot in near:
            total = total + jnp.dot(pr[slot], win[slot, :, columns], preferred_element_type=F32)
        gu[:, columns] = total
    pass_far(2)
    pass_far(3)
    far = (8 - 8 * core, 8 * core, 1 + 6 * core)
    for i, slot in enumerate(far):
        if i:
            for p in range(PIECES):
                halo_wait(slot, p)
        s, e = tile(slot)
        along = along + pairs(slot, s, e)
    along = along * (1.0 / SCALE)
    for half in (0, 1):
        x_wait(slot_rows(2, core, half), 3, half)
    x_copy(slot_rows(2, core), 9, 6, 0, sibling)

    for step in (2, 1, 3, 0):
        x_to = wrap(x_me + step, NX)
        columns = pl.ds(pl.multiple_of(x_to * 256, 256), 256)
        total = gu[:, columns]
        for slot in far:
            total = total + jnp.dot(pr[slot], win[slot, :, columns], preferred_element_type=F32)
        grad = ((total - zn[:, columns] * along) * rnorm).astype(BF16)
        for which in (0, 1):
            gzs[x_to * 2 + which] = grad[:, which * SLICE : (which + 1) * SLICE]
        for which in (0, 1):
            if step == 0 and which == 0:
                target, device = x_me * 2 + 1 - core, sibling
            elif step == 0:
                continue
            else:
                target, device = x_to * 2 + which, x_peer(step, which)
            copy = remote(
                gzs.at[target], gzg.at[own_rows, :], g_send.at[2 * step + which], g_recv.at[own_x], device
            )
            copy.start()
            sends.append(copy)
    gzg[own_rows, :] = gzs[own_x]

    x_wait(slot_rows(0, 1 - core), 0, 0)
    x_wait(slot_rows(-1, 1 - core), 4, 0)
    x_wait(slot_rows(1, 1 - core), 5, 0)
    x_wait(slot_rows(2, 1 - core), 6, 0)
    for step, which in ((0, 1 - core), (1, 0), (1, 1), (3, 0), (3, 1), (2, 0), (2, 1)):
        source = wrap(x_me + step, NX) * 2 + which
        rows = slot_rows(step, which)
        remote(gzs.at[0], gzg.at[rows, :], g_send.at[0], g_recv.at[source], sibling).wait_recv()

    def y_self(yl, which):
        return jnp.logical_and(core == yh_me, jnp.logical_and(yl_me == yl, core == which))

    def y_copy(yl, which, part_no):
        rows = pl.ds(yl * (2 * YROWS) + which * YROWS + part_no * YPART, YPART)
        return remote(
            part.at[rows, :], yb.at[part_no, y_me], y_send.at[part_no, yl, which], y_recv.at[part_no, y_me],
            ((yl * NZ + z_me) * 2 + which, x_me * NYH + core),
        )

    def y_start(yl, which):
        @pl.when(jnp.logical_not(y_self(yl, which)))
        def _():
            for part_no in (0, 1):
                y_copy(yl, which, part_no).start()

        @pl.when(y_self(yl, which))
        def _():
            for part_no in (0, 1):
                start = yl * (2 * YROWS) + which * YROWS + part_no * YPART
                yb[part_no, y_me] = part[start : start + YPART, :]

    grads = jnp.transpose(gzg[...])
    started = 0
    for n in range(E // 256):
        piece = jnp.dot(grads, embg[:, n * 256 : (n + 1) * 256], preferred_element_type=F32)
        part[n * 256 : (n + 1) * 256, :] = jnp.transpose(piece).astype(YTYPE)
        while (started + 1) * YROWS <= (n + 1) * 256:
            y_start(started // 2, started % 2)
            started += 1

    def z_copy(i, which):
        return remote(
            zs.at[i * 2 + which], zb.at[z_me], z_send.at[i, which], z_recv.at[z_me],
            ((yl_me * NZ + core * (NZ // 2) + i) * 2 + which, grp),
        )

    def z_self(i, which):
        return jnp.logical_and(z_me == core * (NZ // 2) + i, core == which)

    for part_no in (0, 1):
        for src in range(NY):
            @pl.when(jnp.logical_or(y_me != src, core != yh_me))
            def _(src=src):
                remote(
                    yb.at[part_no, src], yb.at[part_no, src],
                    y_send.at[0, 0, 0], y_recv.at[part_no, src], sibling,
                ).wait_recv()

        total = yb[part_no, 0].astype(F32)
        for src in range(1, NY):
            total = total + yb[part_no, src].astype(F32)
        ysum[...] = total
        for i in range(part_no * (NZ // 4), (part_no + 1) * (NZ // 4)):
            for which in (0, 1):
                first = (i % (NZ // 4) * 2 + which) * ZROWS
                for row in range(ZROWS):
                    zs[i * 2 + which, row] = ysum[first + row : first + row + 1, :]

                @pl.when(jnp.logical_not(z_self(i, which)))
                def _(i=i, which=which):
                    z_copy(i, which).start()

                @pl.when(z_self(i, which))
                def _(i=i, which=which):
                    zb[z_me] = zs[i * 2 + which]

    for src in range(NZ):
        @pl.when(jnp.logical_or(z_me != src, core != z_core))
        def _(src=src):
            remote(zb.at[src], zb.at[src], z_send.at[0, 0], z_recv.at[src], sibling).wait_recv()

    total = zb[0]
    for src in range(1, NZ):
        total = total + zb[src]
    for row in range(ZROWS):
        head_ref[row : row + 1, :] = total[row]

    for copy in sends:
        copy.wait_send()
    for yl in range(NYL):
        for which in (0, 1):
            @pl.when(jnp.logical_not(y_self(yl, which)))
            def _(yl=yl, which=which):
                for part_no in (0, 1):
                    y_copy(yl, which, part_no).wait_send()
    for i in range(NZ // 2):
        for which in (0, 1):
            @pl.when(jnp.logical_not(z_self(i, which)))
            def _(i=i, which=which):
                z_copy(i, which).wait_send()


def hand_out(loss_in, head_in, loss_out, head_out, sem):
    first = pltpu.make_async_copy(loss_in, loss_out, sem.at[0])
    second = pltpu.make_async_copy(head_in, head_out, sem.at[1])
    first.start()
    second.start()
    first.wait()
    second.wait()


def on_device(embeddings, proj_weight, labels, flags):
    dma = pltpu.SemaphoreType.DMA
    loss, head = pl.pallas_call(
        kernel,
        out_shape=(
            jax.ShapeDtypeStruct((ROWS,), F32),
            jax.ShapeDtypeStruct((ZROWS, SLICE), F32),
        ),
        in_specs=[pl.BlockSpec(memory_space=pl.ANY)] * 4,
        out_specs=(
            pl.BlockSpec(memory_space=pltpu.VMEM),
            pl.BlockSpec(memory_space=pltpu.VMEM),
        ),
        scratch_shapes=[
            pltpu.VMEM((E, WIDTH), BF16),
            pltpu.VMEM((1536, 128), jnp.int32),
            pltpu.VMEM((1536, 128), jnp.int32),
            pltpu.VMEM((16, 256), F32),
            pltpu.VMEM((2 * NX * ROWS, E), BF16),
            pltpu.VMEM((ROWS, WIDTH), F32),
            pltpu.VMEM((SLOTS, ROWS, WIDTH), BF16),
            pltpu.VMEM((SLOTS, ROWS, ROWS), F32),
            pltpu.VMEM((SLOTS, ROWS, ROWS), F32),
            pltpu.VMEM((SLOTS, ROWS, ROWS), BF16),
            pltpu.VMEM((SLOTS, 8, 256), F32),
            pltpu.VMEM((3, 8, 256), F32),
            pltpu.VMEM((3, 8, 256), F32),
            pltpu.VMEM((ROWS, WIDTH), F32),
            pltpu.VMEM((2 * NX, ROWS, SLICE), BF16),
            pltpu.VMEM((2 * NX * ROWS, SLICE), BF16),
            pltpu.VMEM((E, SLICE), YTYPE),
            pltpu.VMEM((2, NY, YPART, SLICE), YTYPE),
            pltpu.VMEM((YPART, SLICE), F32),
            pltpu.VMEM((NZ, ZROWS, 1, SLICE), F32),
            pltpu.VMEM((NZ, ZROWS, 1, SLICE), F32),
            dma((7,)),
            dma((8, PIECES)),
            dma((SLOTS, PIECES)),
            dma((10,)),
            dma((7, 2)),
            dma((8,)),
            dma((SLOTS,)),
            dma((3,)),
            dma((3,)),
            dma((8,)),
            dma((2 * NX,)),
            dma((2, NYL, 2)),
            dma((2, NY)),
            dma((NZ // 2, 2)),
            dma((NZ,)),
        ],
        compiler_params=pltpu.CompilerParams(
            collective_id=0, has_side_effects=True, vmem_limit_bytes=60 * 2**20
        ),
        name="contrastive_loss_and_head_gradient",
    )(embeddings, proj_weight, labels.reshape(1536, 128), flags.reshape(1536, 128))
    return pl.pallas_call(
        hand_out,
        out_shape=(
            jax.ShapeDtypeStruct((ROWS,), F32),
            jax.ShapeDtypeStruct((ZROWS, SLICE), F32),
        ),
        in_specs=[pl.BlockSpec(memory_space=pl.ANY)] * 2,
        out_specs=(pl.BlockSpec(memory_space=pl.ANY), pl.BlockSpec(memory_space=pl.ANY)),
        scratch_shapes=[dma((2,))],
        compiler_params=pltpu.CompilerParams(vmem_limit_bytes=60 * 2**20),
        name="hand_out",
    )(loss, head)


def solution(mesh):
    return jax.shard_map(
        on_device,
        mesh=mesh,
        in_specs=(P(("blk", "grp"), None), P(), P(), P()),
        out_specs=(P(("blk", "grp")), P("blk", "grp")),
        check_vma=False,
    )
```

```python
import functools

import jax
import jax.numpy as jnp
from jax import lax
from jax.experimental import pallas as pl
from jax.experimental.pallas import tpu as pltpu
from jax.sharding import PartitionSpec as P

MESH = pl.DeviceIdType.MESH
F32 = jnp.float32
BF16 = jnp.bfloat16

NX, NYH, NYL, NZ = 4, 2, 4, 16
NY = NYH * NYL
ROWS, E, WIDTH = 192, 1280, 1024
SLOTS = 9
LABEL_ROWS = 1536
PIECES = 4
PIECE = ROWS // PIECES
HALFROWS = ROWS // 2
SLICE = 128
YROWS = E // NYL // 2
YPART = YROWS // 2
ZROWS = 10
SCALE = 10.0
YTYPE = BF16


def kernel(
    emb_hbm, w_hbm, lab_hbm, flag_hbm, loss_ref, head_ref,
    w_v, lab_v, lw, embg, zn, win, ex, sc, pr, st, gzs, gzg, part, yb, ysum, zs, zb,
    load_sem, halo_send, halo_recv, halo_whole, x_send, x_recv, st_send, st_recv,
    g_send, g_recv, y_send, y_recv, z_send, z_recv,
):
    blk = lax.axis_index("blk")
    grp = lax.axis_index("grp")
    blocks = 2 * NYL * NZ
    core = lax.rem(blk, 2)
    chip = blk // 2
    z_me = lax.rem(chip, NZ)
    yl_me = chip // NZ
    x_me = grp // NYH
    yh_me = lax.rem(grp, NYH)
    y_me = yh_me * NYL + yl_me
    own_x = x_me * 2 + core

    def wrap(value, size):
        return lax.rem(value + size, size)

    def chip_peer(step, which):
        return wrap(chip + step, blocks // 2) * 2 + which, grp

    def x_peer(step, which):
        return chip * 2 + which, wrap(x_me + step, NX) * NYH + yh_me

    sibling = (chip * 2 + 1 - core, grp)
    z_core = z_me // (NZ // 2)

    def remote(src, dst, send, recv, device):
        return pltpu.make_async_remote_copy(
            src_ref=src, dst_ref=dst, send_sem=send, recv_sem=recv, device_id=device, device_id_type=MESH
        )

    own_rows = pl.ds(pl.multiple_of(own_x * ROWS, 16), ROWS)
    loads = [pltpu.make_async_copy(emb_hbm, embg.at[own_rows, :], load_sem.at[0])]
    for n in range(4):
        columns = pl.ds(n * 256, 256)
        loads.append(pltpu.make_async_copy(w_hbm.at[:, columns], w_v.at[:, columns], load_sem.at[1 + n]))

    def label_start(block):
        row = block * 12 + (3 * grp) // 2
        first = jnp.minimum(row - lax.rem(row, 8), LABEL_ROWS - 16)
        return pl.multiple_of(first, 8), row - first

    for slot in range(SLOTS):
        rows = pl.ds(label_start(wrap(blk + slot - 4, blocks))[0], 16)
        loads.append(pltpu.make_async_copy(lab_hbm.at[rows, :], lab_v.at[slot], load_sem.at[5 + slot]))
    rows = pl.ds(label_start(blk)[0], 16)
    loads.append(pltpu.make_async_copy(flag_hbm.at[rows, :], lab_v.at[SLOTS], load_sem.at[5 + SLOTS]))
    for load in loads:
        load.start()

    barrier = pltpu.get_barrier_semaphore()

    def greet(device):
        pl.semaphore_signal(barrier, inc=1, device_id=device, device_id_type=MESH)

    for step in (1, -1, 2, -2, 3, -3, 4, -4):
        greet((wrap(blk + step, blocks), grp))
    for step in (1, 2, 3):
        for which in (0, 1):
            greet(x_peer(step, which))

    def greet_y(y_src, carry):
        @pl.when(jnp.logical_or(y_src != y_me, core != yh_me))
        def _():
            greet(((lax.rem(y_src, NYL) * NZ + z_me) * 2 + yh_me, x_me * NYH + y_src // NYL))
        return carry

    lax.fori_loop(0, NY, greet_y, 0)

    def greet_z(z_src, carry):
        @pl.when(jnp.logical_or(z_src != z_me, core != z_core))
        def _():
            greet(((yl_me * NZ + z_src) * 2 + z_core, grp))
        return carry

    lax.fori_loop(0, NZ, greet_z, 0)

    loads[0].wait()
    greeted = (
        8 + 6 + NY + NZ
        - jnp.where(core == yh_me, 1, 0).astype(jnp.int32)
        - jnp.where(core == z_core, 1, 0).astype(jnp.int32)
    )
    ahead, behind = chip_peer(1, core), chip_peer(-1, core)

    def halo_sem(slot, p):
        if isinstance(slot, int) and slot in (0, 2, 6, 8):
            return halo_recv.at[slot // 2, p]
        return halo_whole.at[slot]

    def halo(src_slot, dst_slot, p, device):
        rows = pl.ds(p * PIECE, PIECE)
        remote(
            win.at[src_slot, rows, :], win.at[dst_slot, rows, :],
            halo_send, halo_sem(dst_slot, p), device,
        ).start()

    def halo_wait(slot, p):
        rows = pl.ds(p * PIECE, PIECE)
        remote(win.at[slot, rows, :], win.at[slot, rows, :], halo_send, halo_sem(slot, p), sibling).wait_recv()

    def halo_wait_all(slot):
        remote(win.at[slot], win.at[slot], halo_send, halo_whole.at[slot], sibling).wait_recv()

    rnorms = []
    for half in (0, 1):
        rows = slice(half * HALFROWS, (half + 1) * HALFROWS)
        emb = embg[pl.ds(pl.multiple_of(own_x * ROWS + half * HALFROWS, 16), HALFROWS), :]
        ssq = jnp.zeros((HALFROWS, 1), F32)
        for n in range(4):
            columns = pl.ds(n * 256, 256)
            if half == 0:
                loads[1 + n].wait()
            zc = jnp.dot(emb, w_v[:, columns], preferred_element_type=F32)
            zn[rows, columns] = zc
            ssq = ssq + jnp.sum(zc * zc, axis=1, keepdims=True)
        rnorms.append(1.0 / jnp.sqrt(ssq + 1e-6))
        for n in range(4):
            columns = pl.ds(n * 256, 256)
            zc = zn[rows, columns] * rnorms[half]
            zn[rows, columns] = zc
            win[4, rows, columns] = zc.astype(BF16)
        if half == 0:
            pl.semaphore_wait(barrier, greeted)
        for p in range(half * (PIECES // 2), (half + 1) * (PIECES // 2)):
            halo(4, 2, p, ahead)
            halo(4, 6, p, behind)
            halo(4, 3 + 2 * core, p, sibling)
    rnorm = jnp.concatenate(rnorms, axis=0)

    right, left = x_peer(1, core), x_peer(-1, core)

    def slot_rows(x_step, which, half=None):
        start = (wrap(x_me + x_step, NX) * 2 + which) * ROWS
        if half is None:
            return pl.ds(pl.multiple_of(start, 16), ROWS)
        return pl.ds(pl.multiple_of(start + half * HALFROWS, 16), HALFROWS)

    def x_copy(rows, recv, half, device):
        remote(embg.at[rows, :], embg.at[rows, :], x_send, x_recv.at[recv, half], device).start()

    def x_wait(rows, recv, half):
        remote(embg.at[rows, :], embg.at[rows, :], x_send, x_recv.at[recv, half], sibling).wait_recv()

    x_copy(own_rows, 0, 0, sibling)
    for half in (0, 1):
        x_copy(slot_rows(0, core, half), 1, half, right)
    for half in (1, 0):
        x_copy(slot_rows(0, core, half), 2, half, left)

    for load in loads[5:]:
        load.wait()
    odd = lax.rem(grp, 2) == 1

    lw[...] = jnp.zeros_like(lw)
    for slot in range(SLOTS + 1):
        offset = label_start(wrap(blk + slot - 4, blocks) if slot < SLOTS else blk)[1]
        lw[slot : slot + 1, 0:128] = lab_v[slot, pl.ds(offset, 1), :].astype(F32)
        lw[slot : slot + 1, 128:256] = lab_v[slot, pl.ds(offset + 1, 1), :].astype(F32)
    plain = lw[...]
    lw[...] = jnp.where(odd, pltpu.roll(plain, 192, 1), plain)
    turned = jnp.transpose(jnp.concatenate([lw[...], jnp.zeros((112, 256), F32)], axis=0))
    own_lab = turned[:ROWS, 4:5]
    own_w = jnp.where(turned[:ROWS, SLOTS : SLOTS + 1] == 1.0, 0.5, 1.0)
    diagonal = lax.broadcasted_iota(jnp.int32, (ROWS, ROWS), 0) == lax.broadcasted_iota(
        jnp.int32, (ROWS, ROWS), 1
    )

    def same_label(slot, own):
        same = own_lab == lw[pl.ds(slot, 1), :ROWS]
        return jnp.logical_and(same, jnp.logical_not(diagonal)) if own else same

    own_unit = win[4]

    def scores(slot, sums, own=False):
        denom, possum, count = sums
        s = SCALE * lax.dot_general(
            own_unit, win[slot], (((1,), (1,)), ((), ())), preferred_element_type=F32
        )
        e = jnp.exp(s)
        if own:
            e = jnp.where(diagonal, 0.0, e)
        same = same_label(slot, own)
        ex[slot] = e
        sc[slot] = s
        denom = denom + jnp.sum(e, axis=1, keepdims=True)
        possum = possum + jnp.sum(jnp.where(same, s, 0.0), axis=1, keepdims=True)
        count = count + jnp.sum(jnp.where(same, 1.0, 0.0), axis=1, keepdims=True)
        return denom, possum, count

    nought = jnp.zeros((ROWS, 1), F32)
    sums = scores(4, (nought, nought, nought), own=True)

    for p in range(PIECES):
        halo_wait(2, p)
        halo(2, 0, p, ahead)
        halo(2, 1 + 2 * core, p, sibling)
        halo_wait(6, p)
        halo(6, 8, p, behind)
        halo(6, 5 + 2 * core, p, sibling)
    x_wait(slot_rows(-1, core, 0), 1, 0)
    x_copy(slot_rows(-1, core, 0), 3, 0, right)
    x_wait(slot_rows(1, core, 1), 2, 1)
    x_copy(slot_rows(1, core, 1), 3, 1, left)
    sums = scores(2, sums)
    sums = scores(6, sums)
    for slot in (5 - 2 * core, 3 - 2 * core, 7 - 2 * core):
        halo_wait_all(slot)
        sums = scores(slot, sums)

    @pl.when(core == 0)
    def _():
        for p in range(PIECES):
            halo_wait(8, p)
            halo(8, 7, p, sibling)
        for p in range(PIECES):
            halo_wait(0, p)

    @pl.when(core == 1)
    def _():
        for p in range(PIECES):
            halo_wait(0, p)
            halo(0, 1, p, sibling)
        for p in range(PIECES):
            halo_wait(8, p)

    sums = scores(0, sums)
    sums = scores(8, sums)
    halo_wait_all(1 + 6 * core)
    sums = scores(1 + 6 * core, sums)

    denom, possum, count = sums
    inv_count = 1.0 / jnp.maximum(count, 1.0)
    own_loss = own_w * (jnp.log(denom) - possum * inv_count)
    own_a = (SCALE * own_w) / denom
    own_c = (SCALE * own_w) * inv_count
    lane = lax.broadcasted_iota(jnp.int32, (ROWS, 128), 1)
    columns = jnp.where(lane == 0, own_a, jnp.where(lane == 1, own_c, own_loss))
    flat = jnp.transpose(jnp.concatenate([columns, jnp.zeros((64, 128), F32)], axis=0))
    st[4] = flat[:8]
    loss_ref[...] = flat[2, :ROWS]
    for step in (4, -4, 3, -3, 2, -2, 1, -1):
        remote(st.at[4], st.at[4 - step], st_send, st_recv, (wrap(blk + step, blocks), grp)).start()

    x_wait(slot_rows(-1, core, 1), 1, 1)
    x_copy(slot_rows(-1, core), 4, 0, sibling)
    x_wait(slot_rows(1, core, 0), 2, 0)
    x_copy(slot_rows(1, core), 5, 0, sibling)
    for half in (0, 1):
        x_wait(slot_rows(2, core, half), 3, half)
    x_copy(slot_rows(2, core), 6, 0, sibling)

    def pairs(slot, own=False):
        row = st[slot]
        same = same_label(slot, own)
        value = ex[slot] * (own_a + row[0:1, :ROWS]) - jnp.where(same, own_c + row[1:2, :ROWS], 0.0)
        held = value.astype(BF16)
        pr[slot] = held
        return jnp.sum(held.astype(F32) * sc[slot], axis=1, keepdims=True)

    along = pairs(4, own=True)
    remote(st.at[0:8], st.at[0:8], st_send, st_recv, sibling).wait_recv()
    for slot in (0, 1, 2, 3, 5, 6, 7, 8):
        along = along + pairs(slot)
    along = along * (1.0 / SCALE)

    for step in (2, 1, 3, 0):
        x_to = wrap(x_me + step, NX)
        columns = pl.ds(pl.multiple_of(x_to * 256, 256), 256)
        total = jnp.dot(pr[0], win[0, :, columns], preferred_element_type=F32)
        for slot in range(1, SLOTS):
            total = total + jnp.dot(pr[slot], win[slot, :, columns], preferred_element_type=F32)
        grad = ((total - zn[:, columns] * along) * rnorm).astype(BF16)
        for which in (0, 1):
            gzs[x_to * 2 + which] = grad[:, which * SLICE : (which + 1) * SLICE]
        for which in (0, 1):
            if step == 0 and which == 0:
                target, device = x_me * 2 + 1 - core, sibling
            elif step == 0:
                continue
            else:
                target, device = x_to * 2 + which, x_peer(step, which)
            remote(gzs.at[target], gzg.at[own_rows, :], g_send, g_recv, device).start()
    gzg[own_rows, :] = gzs[own_x]

    x_wait(slot_rows(0, 1 - core), 0, 0)
    x_wait(slot_rows(-1, 1 - core), 4, 0)
    x_wait(slot_rows(1, 1 - core), 5, 0)
    x_wait(slot_rows(2, 1 - core), 6, 0)
    remote(gzs.at[0:7], gzs.at[0:7], g_send, g_recv, sibling).wait_recv()

    def y_self(yl, which):
        return jnp.logical_and(core == yh_me, jnp.logical_and(yl_me == yl, core == which))

    def y_copy(yl, which, part_no):
        rows = pl.ds(yl * (2 * YROWS) + which * YROWS + part_no * YPART, YPART)
        return remote(
            part.at[rows, :], yb.at[part_no, y_me], y_send, y_recv.at[part_no],
            ((yl * NZ + z_me) * 2 + which, x_me * NYH + core),
        )

    def y_start(yl, which):
        @pl.when(jnp.logical_not(y_self(yl, which)))
        def _():
            for part_no in (0, 1):
                y_copy(yl, which, part_no).start()

        @pl.when(y_self(yl, which))
        def _():
            for part_no in (0, 1):
                start = yl * (2 * YROWS) + which * YROWS + part_no * YPART
                yb[part_no, y_me] = part[start : start + YPART, :]

    grads = jnp.transpose(gzg[...])
    started = 0
    for n in range(E // 256):
        piece = jnp.dot(grads, embg[:, n * 256 : (n + 1) * 256], preferred_element_type=F32)
        part[n * 256 : (n + 1) * 256, :] = jnp.transpose(piece).astype(YTYPE)
        while (started + 1) * YROWS <= (n + 1) * 256:
            y_start(started // 2, started % 2)
            started += 1

    def z_copy(i, which):
        return remote(
            zs.at[i * 2 + which], zb.at[z_me], z_send, z_recv,
            ((yl_me * NZ + core * (NZ // 2) + i) * 2 + which, grp),
        )

    def z_self(i, which):
        return jnp.logical_and(z_me == core * (NZ // 2) + i, core == which)

    def y_wait(pieces, part_no):
        rows = yb.at[part_no, 0:pieces]
        remote(rows, rows, y_send, y_recv.at[part_no], sibling).wait_recv()

    for part_no in (0, 1):
        @pl.when(core == yh_me)
        def _(part_no=part_no):
            y_wait(NY - 1, part_no)

        @pl.when(core != yh_me)
        def _(part_no=part_no):
            y_wait(NY, part_no)

        total = yb[part_no, 0].astype(F32)
        for src in range(1, NY):
            total = total + yb[part_no, src].astype(F32)
        ysum[...] = total
        for i in range(part_no * (NZ // 4), (part_no + 1) * (NZ // 4)):
            for which in (0, 1):
                first = (i % (NZ // 4) * 2 + which) * ZROWS
                for row in range(ZROWS):
                    zs[i * 2 + which, row] = ysum[first + row : first + row + 1, :]

                @pl.when(jnp.logical_not(z_self(i, which)))
                def _(i=i, which=which):
                    z_copy(i, which).start()

                @pl.when(z_self(i, which))
                def _(i=i, which=which):
                    zb[z_me] = zs[i * 2 + which]

    @pl.when(core == z_core)
    def _():
        remote(zb.at[1:NZ], zb.at[1:NZ], z_send, z_recv, sibling).wait_recv()

    @pl.when(core != z_core)
    def _():
        remote(zb, zb, z_send, z_recv, sibling).wait_recv()

    total = zb[0]
    for src in range(1, NZ):
        total = total + zb[src]
    for row in range(ZROWS):
        head_ref[row : row + 1, :] = total[row]

    remote(win.at[0:8], win.at[0:8], halo_send, halo_whole.at[0], sibling).wait_send()
    remote(embg.at[0 : 7 * ROWS, :], embg.at[0 : 7 * ROWS, :], x_send, x_recv.at[0, 0], sibling).wait_send()
    remote(st.at[0:8], st.at[0:8], st_send, st_recv, sibling).wait_send()
    remote(gzs.at[0:7], gzs.at[0:7], g_send, g_recv, sibling).wait_send()

    @pl.when(core == yh_me)
    def _():
        remote(yb.at[:, 1:NY], yb.at[:, 1:NY], y_send, y_recv.at[0], sibling).wait_send()

    @pl.when(core != yh_me)
    def _():
        remote(yb, yb, y_send, y_recv.at[0], sibling).wait_send()

    @pl.when(core == z_core)
    def _():
        remote(zs.at[1:NZ], zs.at[1:NZ], z_send, z_recv, sibling).wait_send()

    @pl.when(core != z_core)
    def _():
        remote(zs, zs, z_send, z_recv, sibling).wait_send()


def hand_out(loss_in, head_in, loss_out, head_out, sem):
    first = pltpu.make_async_copy(loss_in, loss_out, sem.at[0])
    second = pltpu.make_async_copy(head_in, head_out, sem.at[1])
    first.start()
    second.start()
    first.wait()
    second.wait()


def on_device(embeddings, proj_weight, labels, flags):
    dma = pltpu.SemaphoreType.DMA
    loss, head = pl.pallas_call(
        kernel,
        out_shape=(
            jax.ShapeDtypeStruct((ROWS,), F32),
            jax.ShapeDtypeStruct((ZROWS, SLICE), F32),
        ),
        in_specs=[pl.BlockSpec(memory_space=pl.ANY)] * 4,
        out_specs=(
            pl.BlockSpec(memory_space=pltpu.VMEM),
            pl.BlockSpec(memory_space=pltpu.VMEM),
        ),
        scratch_shapes=[
            pltpu.VMEM((E, WIDTH), BF16),
            pltpu.VMEM((SLOTS + 1, 16, 128), jnp.int32),
            pltpu.VMEM((16, 256), F32),
            pltpu.VMEM((2 * NX * ROWS, E), BF16),
            pltpu.VMEM((ROWS, WIDTH), F32),
            pltpu.VMEM((SLOTS, ROWS, WIDTH), BF16),
            pltpu.VMEM((SLOTS, ROWS, ROWS), F32),
            pltpu.VMEM((SLOTS, ROWS, ROWS), F32),
            pltpu.VMEM((SLOTS, ROWS, ROWS), BF16),
            pltpu.VMEM((SLOTS, 8, 256), F32),
            pltpu.VMEM((2 * NX, ROWS, SLICE), BF16),
            pltpu.VMEM((2 * NX * ROWS, SLICE), BF16),
            pltpu.VMEM((E, SLICE), YTYPE),
            pltpu.VMEM((2, NY, YPART, SLICE), YTYPE),
            pltpu.VMEM((YPART, SLICE), F32),
            pltpu.VMEM((NZ, ZROWS, 1, SLICE), F32),
            pltpu.VMEM((NZ, ZROWS, 1, SLICE), F32),
            dma((15,)),
            dma,
            dma((5, PIECES)),
            dma((SLOTS,)),
            dma,
            dma((7, 2)),
            dma,
            dma,
            dma,
            dma,
            dma,
            dma((2,)),
            dma,
            dma,
        ],
        compiler_params=pltpu.CompilerParams(
            collective_id=0, has_side_effects=True, vmem_limit_bytes=60 * 2**20
        ),
        name="contrastive_loss_and_head_gradient",
    )(embeddings, proj_weight, labels.reshape(LABEL_ROWS, 128), flags.reshape(LABEL_ROWS, 128))
    return pl.pallas_call(
        hand_out,
        out_shape=(
            jax.ShapeDtypeStruct((ROWS,), F32),
            jax.ShapeDtypeStruct((ZROWS, SLICE), F32),
        ),
        in_specs=[pl.BlockSpec(memory_space=pl.ANY)] * 2,
        out_specs=(pl.BlockSpec(memory_space=pl.ANY), pl.BlockSpec(memory_space=pl.ANY)),
        scratch_shapes=[dma((2,))],
        compiler_params=pltpu.CompilerParams(vmem_limit_bytes=60 * 2**20),
        name="hand_out",
    )(loss, head)


def solution(mesh):
    return jax.shard_map(
        on_device,
        mesh=mesh,
        in_specs=(P(("blk", "grp"), None), P(), P(), P()),
        out_specs=(P(("blk", "grp")), P("blk", "grp")),
        check_vma=False,
    )
```

```python
import functools

import jax
import jax.numpy as jnp
from jax import lax
from jax.experimental import pallas as pl
from jax.experimental.pallas import tpu as pltpu
from jax.sharding import PartitionSpec as P

MESH = pl.DeviceIdType.MESH
F32 = jnp.float32
BF16 = jnp.bfloat16

NX, NYH, NYL, NZ = 4, 2, 4, 16
NY = NYH * NYL
ROWS, E, WIDTH = 192, 1280, 1024
SLOTS = 9
LABEL_ROWS = 1536
PIECES = 4
PIECE = ROWS // PIECES
HALFROWS = ROWS // 2
SLICE = 128
YROWS = E // NYL // 2
YPART = YROWS // 2
ZROWS = 10
SCALE = 10.0
YTYPE = BF16


def kernel(
    emb_hbm, w_hbm, lab_hbm, flag_hbm, loss_ref, head_ref,
    w_v, lab_v, lw, embg, zn, win, ex, sc, pr, st, gzs, gzg, part, yb, ysum, zs, zb,
    load_sem, halo_send, halo_recv, halo_whole, x_send, x_recv, st_send, st_recv,
    g_send, g_recv, y_send, y_recv, z_send, z_recv,
):
    blk = lax.axis_index("blk")
    grp = lax.axis_index("grp")
    blocks = 2 * NYL * NZ
    core = lax.rem(blk, 2)
    chip = blk // 2
    z_me = lax.rem(chip, NZ)
    yl_me = chip // NZ
    x_me = grp // NYH
    yh_me = lax.rem(grp, NYH)
    y_me = yh_me * NYL + yl_me
    own_x = x_me * 2 + core

    def wrap(value, size):
        return lax.rem(value + size, size)

    def chip_peer(step, which):
        return wrap(chip + step, blocks // 2) * 2 + which, grp

    def x_peer(step, which):
        return chip * 2 + which, wrap(x_me + step, NX) * NYH + yh_me

    sibling = (chip * 2 + 1 - core, grp)
    z_core = z_me // (NZ // 2)

    def remote(src, dst, send, recv, device):
        return pltpu.make_async_remote_copy(
            src_ref=src, dst_ref=dst, send_sem=send, recv_sem=recv, device_id=device, device_id_type=MESH
        )

    own_rows = pl.ds(pl.multiple_of(own_x * ROWS, 16), ROWS)
    loads = [pltpu.make_async_copy(emb_hbm, embg.at[own_rows, :], load_sem.at[0])]
    for n in range(4):
        columns = pl.ds(n * 256, 256)
        loads.append(pltpu.make_async_copy(w_hbm.at[:, columns], w_v.at[:, columns], load_sem.at[1 + n]))

    def label_start(block):
        row = block * 12 + (3 * grp) // 2
        first = jnp.minimum(row - lax.rem(row, 8), LABEL_ROWS - 16)
        return pl.multiple_of(first, 8), row - first

    for slot in range(SLOTS):
        rows = pl.ds(label_start(wrap(blk + slot - 4, blocks))[0], 16)
        loads.append(pltpu.make_async_copy(lab_hbm.at[rows, :], lab_v.at[slot], load_sem.at[5 + slot]))
    rows = pl.ds(label_start(blk)[0], 16)
    loads.append(pltpu.make_async_copy(flag_hbm.at[rows, :], lab_v.at[SLOTS], load_sem.at[5 + SLOTS]))
    for load in loads:
        load.start()

    barrier = pltpu.get_barrier_semaphore()

    def greet(device):
        pl.semaphore_signal(barrier, inc=1, device_id=device, device_id_type=MESH)

    for step in (1, -1, 2, -2, 3, -3, 4, -4):
        greet((wrap(blk + step, blocks), grp))
    for step in (1, 2, 3):
        for which in (0, 1):
            greet(x_peer(step, which))

    def greet_y(y_src, carry):
        @pl.when(jnp.logical_or(y_src != y_me, core != yh_me))
        def _():
            greet(((lax.rem(y_src, NYL) * NZ + z_me) * 2 + yh_me, x_me * NYH + y_src // NYL))
        return carry

    lax.fori_loop(0, NY, greet_y, 0)

    def greet_z(z_src, carry):
        @pl.when(jnp.logical_or(z_src != z_me, core != z_core))
        def _():
            greet(((yl_me * NZ + z_src) * 2 + z_core, grp))
        return carry

    lax.fori_loop(0, NZ, greet_z, 0)

    loads[0].wait()
    greeted = (
        8 + 6 + NY + NZ
        - jnp.where(core == yh_me, 1, 0).astype(jnp.int32)
        - jnp.where(core == z_core, 1, 0).astype(jnp.int32)
    )
    ahead, behind = chip_peer(1, core), chip_peer(-1, core)

    def halo_sem(slot, p):
        if isinstance(slot, int) and slot in (0, 2, 6, 8):
            return halo_recv.at[slot // 2, p]
        return halo_whole.at[slot]

    def halo(src_slot, dst_slot, p, device):
        rows = pl.ds(p * PIECE, PIECE)
        remote(
            win.at[src_slot, rows, :], win.at[dst_slot, rows, :],
            halo_send, halo_sem(dst_slot, p), device,
        ).start()

    def halo_wait(slot, p):
        rows = pl.ds(p * PIECE, PIECE)
        remote(win.at[slot, rows, :], win.at[slot, rows, :], halo_send, halo_sem(slot, p), sibling).wait_recv()

    def halo_wait_all(slot):
        remote(win.at[slot], win.at[slot], halo_send, halo_whole.at[slot], sibling).wait_recv()

    rnorms = []
    for half in (0, 1):
        rows = slice(half * HALFROWS, (half + 1) * HALFROWS)
        emb = embg[pl.ds(pl.multiple_of(own_x * ROWS + half * HALFROWS, 16), HALFROWS), :]
        ssq = jnp.zeros((HALFROWS, 1), F32)
        for n in range(4):
            columns = pl.ds(n * 256, 256)
            if half == 0:
                loads[1 + n].wait()
            zc = jnp.dot(emb, w_v[:, columns], preferred_element_type=F32)
            zn[rows, columns] = zc
            ssq = ssq + jnp.sum(zc * zc, axis=1, keepdims=True)
        rnorms.append(1.0 / jnp.sqrt(ssq + 1e-6))
        for n in range(4):
            columns = pl.ds(n * 256, 256)
            zc = zn[rows, columns] * rnorms[half]
            zn[rows, columns] = zc
            win[4, rows, columns] = zc.astype(BF16)
        if half == 0:
            pl.semaphore_wait(barrier, greeted)
        for p in range(half * (PIECES // 2), (half + 1) * (PIECES // 2)):
            halo(4, 2, p, ahead)
            halo(4, 6, p, behind)
            halo(4, 3 + 2 * core, p, sibling)
    rnorm = jnp.concatenate(rnorms, axis=0)

    right, left = x_peer(1, core), x_peer(-1, core)

    def slot_rows(x_step, which, half=None):
        start = (wrap(x_me + x_step, NX) * 2 + which) * ROWS
        if half is None:
            return pl.ds(pl.multiple_of(start, 16), ROWS)
        return pl.ds(pl.multiple_of(start + half * HALFROWS, 16), HALFROWS)

    def x_copy(rows, recv, half, device):
        remote(embg.at[rows, :], embg.at[rows, :], x_send, x_recv.at[recv, half], device).start()

    def x_wait(rows, recv, half):
        remote(embg.at[rows, :], embg.at[rows, :], x_send, x_recv.at[recv, half], sibling).wait_recv()

    x_copy(own_rows, 0, 0, sibling)
    for half in (0, 1):
        x_copy(slot_rows(0, core, half), 1, half, right)
    for half in (1, 0):
        x_copy(slot_rows(0, core, half), 2, half, left)

    for load in loads[5:]:
        load.wait()
    odd = lax.rem(grp, 2) == 1

    lw[...] = jnp.zeros_like(lw)
    for slot in range(SLOTS + 1):
        offset = label_start(wrap(blk + slot - 4, blocks) if slot < SLOTS else blk)[1]
        lw[slot : slot + 1, 0:128] = lab_v[slot, pl.ds(offset, 1), :].astype(F32)
        lw[slot : slot + 1, 128:256] = lab_v[slot, pl.ds(offset + 1, 1), :].astype(F32)
    plain = lw[...]
    lw[...] = jnp.where(odd, pltpu.roll(plain, 192, 1), plain)
    turned = jnp.transpose(jnp.concatenate([lw[...], jnp.zeros((112, 256), F32)], axis=0))
    own_lab = turned[:ROWS, 4:5]
    own_w = jnp.where(turned[:ROWS, SLOTS : SLOTS + 1] == 1.0, 0.5, 1.0)
    diagonal = lax.broadcasted_iota(jnp.int32, (ROWS, ROWS), 0) == lax.broadcasted_iota(
        jnp.int32, (ROWS, ROWS), 1
    )

    def same_label(slot, own):
        same = own_lab == lw[pl.ds(slot, 1), :ROWS]
        return jnp.logical_and(same, jnp.logical_not(diagonal)) if own else same

    own_unit = win[4]

    def scores(slot, sums, own=False):
        denom, possum, count = sums
        s = SCALE * lax.dot_general(
            own_unit, win[slot], (((1,), (1,)), ((), ())), preferred_element_type=F32
        )
        e = jnp.exp(s)
        if own:
            e = jnp.where(diagonal, 0.0, e)
        same = same_label(slot, own)
        ex[slot] = e
        sc[slot] = s
        denom = denom + jnp.sum(e, axis=1, keepdims=True)
        possum = possum + jnp.sum(jnp.where(same, s, 0.0), axis=1, keepdims=True)
        count = count + jnp.sum(jnp.where(same, 1.0, 0.0), axis=1, keepdims=True)
        return denom, possum, count

    nought = jnp.zeros((ROWS, 1), F32)
    sums = scores(4, (nought, nought, nought), own=True)

    for p in range(PIECES):
        halo_wait(2, p)
        halo(2, 0, p, ahead)
        halo(2, 1 + 2 * core, p, sibling)
        halo_wait(6, p)
        halo(6, 8, p, behind)
        halo(6, 5 + 2 * core, p, sibling)
    x_wait(slot_rows(-1, core, 0), 1, 0)
    x_copy(slot_rows(-1, core, 0), 3, 0, right)
    x_wait(slot_rows(1, core, 1), 2, 1)
    x_copy(slot_rows(1, core, 1), 3, 1, left)
    sums = scores(2, sums)
    sums = scores(6, sums)
    for slot in (5 - 2 * core, 3 - 2 * core, 7 - 2 * core):
        halo_wait_all(slot)
        sums = scores(slot, sums)

    @pl.when(core == 0)
    def _():
        for p in range(PIECES):
            halo_wait(8, p)
            halo(8, 7, p, sibling)
        for p in range(PIECES):
            halo_wait(0, p)

    @pl.when(core == 1)
    def _():
        for p in range(PIECES):
            halo_wait(0, p)
            halo(0, 1, p, sibling)
        for p in range(PIECES):
            halo_wait(8, p)

    sums = scores(0, sums)
    sums = scores(8, sums)
    halo_wait_all(1 + 6 * core)
    sums = scores(1 + 6 * core, sums)

    denom, possum, count = sums
    inv_count = 1.0 / jnp.maximum(count, 1.0)
    own_loss = own_w * (jnp.log(denom) - possum * inv_count)
    own_a = (SCALE * own_w) / denom
    own_c = (SCALE * own_w) * inv_count
    lane = lax.broadcasted_iota(jnp.int32, (ROWS, 128), 1)
    columns = jnp.where(lane == 0, own_a, jnp.where(lane == 1, own_c, own_loss))
    flat = jnp.transpose(jnp.concatenate([columns, jnp.zeros((64, 128), F32)], axis=0))
    st[4] = flat[:8]
    loss_ref[...] = flat[2, :ROWS]
    for step in (4, -4, 3, -3, 2, -2, 1, -1):
        remote(st.at[4], st.at[4 - step], st_send, st_recv, (wrap(blk + step, blocks), grp)).start()

    x_wait(slot_rows(-1, core, 1), 1, 1)
    x_copy(slot_rows(-1, core), 4, 0, sibling)
    x_wait(slot_rows(1, core, 0), 2, 0)
    x_copy(slot_rows(1, core), 5, 0, sibling)
    for half in (0, 1):
        x_wait(slot_rows(2, core, half), 3, half)
    x_copy(slot_rows(2, core), 6, 0, sibling)

    def pairs(slot, own=False):
        row = st[slot]
        same = same_label(slot, own)
        value = ex[slot] * (own_a + row[0:1, :ROWS]) - jnp.where(same, own_c + row[1:2, :ROWS], 0.0)
        held = value.astype(BF16)
        pr[slot] = held
        return jnp.sum(held.astype(F32) * sc[slot], axis=1, keepdims=True)

    along = pairs(4, own=True)
    remote(st.at[0:8], st.at[0:8], st_send, st_recv, sibling).wait_recv()
    for slot in (0, 1, 2, 3, 5, 6, 7, 8):
        along = along + pairs(slot)
    along = along * (1.0 / SCALE)

    for step in (2, 1, 3, 0):
        x_to = wrap(x_me + step, NX)
        columns = pl.ds(pl.multiple_of(x_to * 256, 256), 256)
        total = jnp.dot(pr[0], win[0, :, columns], preferred_element_type=F32)
        for slot in range(1, SLOTS):
            total = total + jnp.dot(pr[slot], win[slot, :, columns], preferred_element_type=F32)
        grad = ((total - zn[:, columns] * along) * rnorm).astype(BF16)
        for which in (0, 1):
            gzs[x_to * 2 + which] = grad[:, which * SLICE : (which + 1) * SLICE]
        for which in (0, 1):
            if step == 0 and which == 0:
                target, device = x_me * 2 + 1 - core, sibling
            elif step == 0:
                continue
            else:
                target, device = x_to * 2 + which, x_peer(step, which)
            remote(gzs.at[target], gzg.at[own_rows, :], g_send, g_recv, device).start()
    gzg[own_rows, :] = gzs[own_x]

    x_wait(slot_rows(0, 1 - core), 0, 0)
    x_wait(slot_rows(-1, 1 - core), 4, 0)
    x_wait(slot_rows(1, 1 - core), 5, 0)
    x_wait(slot_rows(2, 1 - core), 6, 0)
    remote(gzs.at[0:7], gzs.at[0:7], g_send, g_recv, sibling).wait_recv()

    def y_self(yl, which):
        return jnp.logical_and(core == yh_me, jnp.logical_and(yl_me == yl, core == which))

    def y_copy(yl, which, part_no):
        rows = pl.ds(yl * (2 * YROWS) + which * YROWS + part_no * YPART, YPART)
        return remote(
            part.at[rows, :], yb.at[part_no, y_me], y_send, y_recv.at[part_no],
            ((yl * NZ + z_me) * 2 + which, x_me * NYH + core),
        )

    def y_start(yl, which, part_no):
        @pl.when(jnp.logical_not(y_self(yl, which)))
        def _():
            y_copy(yl, which, part_no).start()

        @pl.when(y_self(yl, which))
        def _():
            start = yl * (2 * YROWS) + which * YROWS + part_no * YPART
            yb[part_no, y_me] = part[start : start + YPART, :]

    grads = jnp.transpose(gzg[...])
    started = 0
    for n in range(E // 256):
        piece = jnp.dot(grads, embg[:, n * 256 : (n + 1) * 256], preferred_element_type=F32)
        part[n * 256 : (n + 1) * 256, :] = jnp.transpose(piece).astype(YTYPE)
        while (started + 1) * YROWS <= (n + 1) * 256:
            y_start(started // 2, started % 2, 0)
            started += 1
    for i in range(2 * NYL):
        y_start(i // 2, i % 2, 1)

    def z_copy(i, which):
        return remote(
            zs.at[i * 2 + which], zb.at[z_me], z_send, z_recv,
            ((yl_me * NZ + core * (NZ // 2) + i) * 2 + which, grp),
        )

    def z_self(i, which):
        return jnp.logical_and(z_me == core * (NZ // 2) + i, core == which)

    def y_wait(pieces, part_no):
        rows = yb.at[part_no, 0:pieces]
        remote(rows, rows, y_send, y_recv.at[part_no], sibling).wait_recv()

    for part_no in (0, 1):
        @pl.when(core == yh_me)
        def _(part_no=part_no):
            y_wait(NY - 1, part_no)

        @pl.when(core != yh_me)
        def _(part_no=part_no):
            y_wait(NY, part_no)

        total = yb[part_no, 0].astype(F32)
        for src in range(1, NY):
            total = total + yb[part_no, src].astype(F32)
        ysum[...] = total
        for i in range(part_no * (NZ // 4), (part_no + 1) * (NZ // 4)):
            for which in (0, 1):
                first = (i % (NZ // 4) * 2 + which) * ZROWS
                for row in range(ZROWS):
                    zs[i * 2 + which, row] = ysum[first + row : first + row + 1, :]

                @pl.when(jnp.logical_not(z_self(i, which)))
                def _(i=i, which=which):
                    z_copy(i, which).start()

                @pl.when(z_self(i, which))
                def _(i=i, which=which):
                    zb[z_me] = zs[i * 2 + which]

    @pl.when(core == z_core)
    def _():
        remote(zb.at[1:NZ], zb.at[1:NZ], z_send, z_recv, sibling).wait_recv()

    @pl.when(core != z_core)
    def _():
        remote(zb, zb, z_send, z_recv, sibling).wait_recv()

    total = zb[0]
    for src in range(1, NZ):
        total = total + zb[src]
    for row in range(ZROWS):
        head_ref[row : row + 1, :] = total[row]

    remote(win.at[0:8], win.at[0:8], halo_send, halo_whole.at[0], sibling).wait_send()
    remote(embg.at[0 : 7 * ROWS, :], embg.at[0 : 7 * ROWS, :], x_send, x_recv.at[0, 0], sibling).wait_send()
    remote(st.at[0:8], st.at[0:8], st_send, st_recv, sibling).wait_send()
    remote(gzs.at[0:7], gzs.at[0:7], g_send, g_recv, sibling).wait_send()

    @pl.when(core == yh_me)
    def _():
        remote(yb.at[:, 1:NY], yb.at[:, 1:NY], y_send, y_recv.at[0], sibling).wait_send()

    @pl.when(core != yh_me)
    def _():
        remote(yb, yb, y_send, y_recv.at[0], sibling).wait_send()

    @pl.when(core == z_core)
    def _():
        remote(zs.at[1:NZ], zs.at[1:NZ], z_send, z_recv, sibling).wait_send()

    @pl.when(core != z_core)
    def _():
        remote(zs, zs, z_send, z_recv, sibling).wait_send()


def hand_out(loss_in, head_in, loss_out, head_out, sem):
    first = pltpu.make_async_copy(loss_in, loss_out, sem.at[0])
    second = pltpu.make_async_copy(head_in, head_out, sem.at[1])
    first.start()
    second.start()
    first.wait()
    second.wait()


def on_device(embeddings, proj_weight, labels, flags):
    dma = pltpu.SemaphoreType.DMA
    loss, head = pl.pallas_call(
        kernel,
        out_shape=(pltpu.VMEM((ROWS,), F32), pltpu.VMEM((ZROWS, SLICE), F32)),
        in_specs=[pl.BlockSpec(memory_space=pl.ANY)] * 4,
        out_specs=(
            pl.BlockSpec(memory_space=pltpu.VMEM),
            pl.BlockSpec(memory_space=pltpu.VMEM),
        ),
        scratch_shapes=[
            pltpu.VMEM((E, WIDTH), BF16),
            pltpu.VMEM((SLOTS + 1, 16, 128), jnp.int32),
            pltpu.VMEM((16, 256), F32),
            pltpu.VMEM((2 * NX * ROWS, E), BF16),
            pltpu.VMEM((ROWS, WIDTH), F32),
            pltpu.VMEM((SLOTS, ROWS, WIDTH), BF16),
            pltpu.VMEM((SLOTS, ROWS, ROWS), F32),
            pltpu.VMEM((SLOTS, ROWS, ROWS), F32),
            pltpu.VMEM((SLOTS, ROWS, ROWS), BF16),
            pltpu.VMEM((SLOTS, 8, 256), F32),
            pltpu.VMEM((2 * NX, ROWS, SLICE), BF16),
            pltpu.VMEM((2 * NX * ROWS, SLICE), BF16),
            pltpu.VMEM((E, SLICE), YTYPE),
            pltpu.VMEM((2, NY, YPART, SLICE), YTYPE),
            pltpu.VMEM((YPART, SLICE), F32),
            pltpu.VMEM((NZ, ZROWS, 1, SLICE), F32),
            pltpu.VMEM((NZ, ZROWS, 1, SLICE), F32),
            dma((15,)),
            dma,
            dma((5, PIECES)),
            dma((SLOTS,)),
            dma,
            dma((7, 2)),
            dma,
            dma,
            dma,
            dma,
            dma,
            dma((2,)),
            dma,
            dma,
        ],
        compiler_params=pltpu.CompilerParams(
            collective_id=0, has_side_effects=True, vmem_limit_bytes=60 * 2**20
        ),
        name="contrastive_loss_and_head_gradient",
    )(embeddings, proj_weight, labels.reshape(LABEL_ROWS, 128), flags.reshape(LABEL_ROWS, 128))
    return pl.pallas_call(
        hand_out,
        out_shape=(
            jax.ShapeDtypeStruct((ROWS,), F32),
            jax.ShapeDtypeStruct((ZROWS, SLICE), F32),
        ),
        in_specs=[pl.BlockSpec(memory_space=pltpu.VMEM)] * 2,
        out_specs=(pl.BlockSpec(memory_space=pl.ANY), pl.BlockSpec(memory_space=pl.ANY)),
        scratch_shapes=[dma((2,))],
        compiler_params=pltpu.CompilerParams(vmem_limit_bytes=2**20),
        name="hand_out",
    )(loss, head)


def solution(mesh):
    return jax.shard_map(
        on_device,
        mesh=mesh,
        in_specs=(P(("blk", "grp"), None), P(), P(), P()),
        out_specs=(P(("blk", "grp")), P("blk", "grp")),
        check_vma=False,
    )
```

```python
import functools

import jax
import jax.numpy as jnp
from jax import lax
from jax.experimental import pallas as pl
from jax.experimental.pallas import tpu as pltpu
from jax.sharding import PartitionSpec as P

MESH = pl.DeviceIdType.MESH
F32 = jnp.float32
BF16 = jnp.bfloat16

NX, NYH, NYL, NZ = 4, 2, 4, 16
NY = NYH * NYL
ROWS, E, WIDTH = 192, 1280, 1024
SLOTS = 9
LABEL_ROWS = 1536
PIECES = 4
PIECE = ROWS // PIECES
HALFROWS = ROWS // 2
SLICE = 128
YROWS = E // NYL // 2
YPART = YROWS // 2
ZROWS = 10
SCALE = 10.0
YTYPE = BF16


def kernel(
    emb_hbm, w_hbm, lab_hbm, flag_hbm, loss_ref, head_ref,
    w_v, lab_v, lw, embg, zn, win, ex, sc, pr, st, gzs, gzg, part, yb, ysum, zs, zb,
    load_sem, halo_send, halo_recv, halo_whole, x_send, x_recv, st_send, st_recv,
    g_send, g_recv, y_send, y_recv, z_send, z_recv,
):
    blk = lax.axis_index("blk")
    grp = lax.axis_index("grp")
    blocks = 2 * NYL * NZ
    core = lax.rem(blk, 2)
    chip = blk // 2
    z_me = lax.rem(chip, NZ)
    yl_me = chip // NZ
    x_me = grp // NYH
    yh_me = lax.rem(grp, NYH)
    y_me = yh_me * NYL + yl_me
    own_x = x_me * 2 + core

    def wrap(value, size):
        return lax.rem(value + size, size)

    def chip_peer(step, which):
        return wrap(chip + step, blocks // 2) * 2 + which, grp

    def x_peer(step, which):
        return chip * 2 + which, wrap(x_me + step, NX) * NYH + yh_me

    sibling = (chip * 2 + 1 - core, grp)
    z_core = z_me // (NZ // 2)

    def remote(src, dst, send, recv, device):
        return pltpu.make_async_remote_copy(
            src_ref=src, dst_ref=dst, send_sem=send, recv_sem=recv, device_id=device, device_id_type=MESH
        )

    own_rows = pl.ds(pl.multiple_of(own_x * ROWS, 16), ROWS)
    loads = [pltpu.make_async_copy(emb_hbm, embg.at[own_rows, :], load_sem.at[0])]
    for n in range(4):
        columns = pl.ds(n * 256, 256)
        loads.append(pltpu.make_async_copy(w_hbm.at[:, columns], w_v.at[:, columns], load_sem.at[1 + n]))
    for load in loads:
        load.start()

    barrier = pltpu.get_barrier_semaphore()

    def greet(device):
        pl.semaphore_signal(barrier, inc=1, device_id=device, device_id_type=MESH)

    for step in (8, 7, 9, 6, 10, 5, 11, 4, 12, 3, 13, 2, 14, 1, 15):
        greet(((yl_me * NZ + wrap(z_me + step, NZ)) * 2 + z_core, grp))
    for step in (4, 3, 5, 2, 6, 1, 7):
        y_src = wrap(y_me + step, NY)
        greet(((lax.rem(y_src, NYL) * NZ + z_me) * 2 + yh_me, x_me * NYH + y_src // NYL))
    for step in (2, 1, 3):
        for which in (0, 1):
            greet(x_peer(step, which))
    for step in (4, -4, 3, -3, 2, -2, 1, -1):
        greet((wrap(blk + step, blocks), grp))

    @pl.when(core != z_core)
    def _():
        greet(sibling)

    @pl.when(core != yh_me)
    def _():
        greet(sibling)

    def label_start(block):
        row = block * 12 + (3 * grp) // 2
        first = jnp.minimum(row - lax.rem(row, 8), LABEL_ROWS - 16)
        return pl.multiple_of(first, 8), row - first

    for slot in range(SLOTS):
        rows = pl.ds(label_start(wrap(blk + slot - 4, blocks))[0], 16)
        loads.append(pltpu.make_async_copy(lab_hbm.at[rows, :], lab_v.at[slot], load_sem.at[5 + slot]))
    rows = pl.ds(label_start(blk)[0], 16)
    loads.append(pltpu.make_async_copy(flag_hbm.at[rows, :], lab_v.at[SLOTS], load_sem.at[5 + SLOTS]))
    for load in loads[5:]:
        load.start()

    loads[0].wait()
    greeted = (
        8 + 6 + NY + NZ
        - jnp.where(core == yh_me, 1, 0).astype(jnp.int32)
        - jnp.where(core == z_core, 1, 0).astype(jnp.int32)
    )
    ahead, behind = chip_peer(1, core), chip_peer(-1, core)

    def halo_sem(slot, p):
        if isinstance(slot, int) and slot in (0, 2, 6, 8):
            return halo_recv.at[slot // 2, p]
        return halo_whole.at[slot]

    def halo(src_slot, dst_slot, p, device):
        rows = pl.ds(p * PIECE, PIECE)
        remote(
            win.at[src_slot, rows, :], win.at[dst_slot, rows, :],
            halo_send, halo_sem(dst_slot, p), device,
        ).start()

    def halo_wait(slot, p):
        rows = pl.ds(p * PIECE, PIECE)
        remote(win.at[slot, rows, :], win.at[slot, rows, :], halo_send, halo_sem(slot, p), sibling).wait_recv()

    def halo_wait_all(slot):
        remote(win.at[slot], win.at[slot], halo_send, halo_whole.at[slot], sibling).wait_recv()

    rnorms = []
    for half in (0, 1):
        rows = slice(half * HALFROWS, (half + 1) * HALFROWS)
        emb = embg[pl.ds(pl.multiple_of(own_x * ROWS + half * HALFROWS, 16), HALFROWS), :]
        ssq = jnp.zeros((HALFROWS, 1), F32)
        for n in range(4):
            columns = pl.ds(n * 256, 256)
            if half == 0:
                loads[1 + n].wait()
            zc = jnp.dot(emb, w_v[:, columns], preferred_element_type=F32)
            zn[rows, columns] = zc
            ssq = ssq + jnp.sum(zc * zc, axis=1, keepdims=True)
        rnorms.append(1.0 / jnp.sqrt(ssq + 1e-6))
        for n in range(4):
            columns = pl.ds(n * 256, 256)
            zc = zn[rows, columns] * rnorms[half]
            zn[rows, columns] = zc
            win[4, rows, columns] = zc.astype(BF16)
        if half == 0:
            pl.semaphore_wait(barrier, greeted)
        for p in range(half * (PIECES // 2), (half + 1) * (PIECES // 2)):
            halo(4, 2, p, ahead)
            halo(4, 6, p, behind)
            halo(4, 3 + 2 * core, p, sibling)
    rnorm = jnp.concatenate(rnorms, axis=0)

    right, left = x_peer(1, core), x_peer(-1, core)

    def slot_rows(x_step, which, half=None):
        start = (wrap(x_me + x_step, NX) * 2 + which) * ROWS
        if half is None:
            return pl.ds(pl.multiple_of(start, 16), ROWS)
        return pl.ds(pl.multiple_of(start + half * HALFROWS, 16), HALFROWS)

    def x_copy(rows, recv, half, device):
        remote(embg.at[rows, :], embg.at[rows, :], x_send, x_recv.at[recv, half], device).start()

    def x_wait(rows, recv, half):
        remote(embg.at[rows, :], embg.at[rows, :], x_send, x_recv.at[recv, half], sibling).wait_recv()

    x_copy(own_rows, 0, 0, sibling)
    for half in (0, 1):
        x_copy(slot_rows(0, core, half), 1, half, right)
    for half in (1, 0):
        x_copy(slot_rows(0, core, half), 2, half, left)

    for load in loads[5:]:
        load.wait()
    odd = lax.rem(grp, 2) == 1

    lw[...] = jnp.zeros_like(lw)
    for slot in range(SLOTS + 1):
        offset = label_start(wrap(blk + slot - 4, blocks) if slot < SLOTS else blk)[1]
        lw[slot : slot + 1, 0:128] = lab_v[slot, pl.ds(offset, 1), :].astype(F32)
        lw[slot : slot + 1, 128:256] = lab_v[slot, pl.ds(offset + 1, 1), :].astype(F32)
    plain = lw[...]
    lw[...] = jnp.where(odd, pltpu.roll(plain, 192, 1), plain)
    turned = jnp.transpose(jnp.concatenate([lw[...], jnp.zeros((112, 256), F32)], axis=0))
    own_lab = turned[:ROWS, 4:5]
    own_w = jnp.where(turned[:ROWS, SLOTS : SLOTS + 1] == 1.0, 0.5, 1.0)
    diagonal = lax.broadcasted_iota(jnp.int32, (ROWS, ROWS), 0) == lax.broadcasted_iota(
        jnp.int32, (ROWS, ROWS), 1
    )

    def same_label(slot, own):
        same = own_lab == lw[pl.ds(slot, 1), :ROWS]
        return jnp.logical_and(same, jnp.logical_not(diagonal)) if own else same

    own_unit = win[4]

    def scores(slot, sums, own=False):
        denom, possum, count = sums
        s = SCALE * lax.dot_general(
            own_unit, win[slot], (((1,), (1,)), ((), ())), preferred_element_type=F32
        )
        e = jnp.exp(s)
        if own:
            e = jnp.where(diagonal, 0.0, e)
        same = same_label(slot, own)
        ex[slot] = e
        sc[slot] = s
        denom = denom + jnp.sum(e, axis=1, keepdims=True)
        possum = possum + jnp.sum(jnp.where(same, s, 0.0), axis=1, keepdims=True)
        count = count + jnp.sum(jnp.where(same, 1.0, 0.0), axis=1, keepdims=True)
        return denom, possum, count

    nought = jnp.zeros((ROWS, 1), F32)
    sums = scores(4, (nought, nought, nought), own=True)

    for p in range(PIECES):
        halo_wait(2, p)
        halo(2, 0, p, ahead)
        halo(2, 1 + 2 * core, p, sibling)
        halo_wait(6, p)
        halo(6, 8, p, behind)
        halo(6, 5 + 2 * core, p, sibling)
    x_wait(slot_rows(-1, core, 0), 1, 0)
    x_copy(slot_rows(-1, core, 0), 3, 0, right)
    x_wait(slot_rows(1, core, 1), 2, 1)
    x_copy(slot_rows(1, core, 1), 3, 1, left)
    sums = scores(2, sums)
    sums = scores(6, sums)
    for slot in (5 - 2 * core, 3 - 2 * core, 7 - 2 * core):
        halo_wait_all(slot)
        sums = scores(slot, sums)

    @pl.when(core == 0)
    def _():
        for p in range(PIECES):
            halo_wait(8, p)
            halo(8, 7, p, sibling)
        for p in range(PIECES):
            halo_wait(0, p)

    @pl.when(core == 1)
    def _():
        for p in range(PIECES):
            halo_wait(0, p)
            halo(0, 1, p, sibling)
        for p in range(PIECES):
            halo_wait(8, p)

    sums = scores(0, sums)
    sums = scores(8, sums)
    halo_wait_all(1 + 6 * core)
    sums = scores(1 + 6 * core, sums)

    denom, possum, count = sums
    inv_count = 1.0 / jnp.maximum(count, 1.0)
    own_loss = own_w * (jnp.log(denom) - possum * inv_count)
    own_a = (SCALE * own_w) / denom
    own_c = (SCALE * own_w) * inv_count
    lane = lax.broadcasted_iota(jnp.int32, (ROWS, 128), 1)
    columns = jnp.where(lane == 0, own_a, jnp.where(lane == 1, own_c, own_loss))
    flat = jnp.transpose(jnp.concatenate([columns, jnp.zeros((64, 128), F32)], axis=0))
    st[4] = flat[:8]
    loss_ref[...] = flat[2, :ROWS]
    for step in (4, -4, 3, -3, 2, -2, 1, -1):
        remote(st.at[4], st.at[4 - step], st_send, st_recv, (wrap(blk + step, blocks), grp)).start()

    x_wait(slot_rows(-1, core, 1), 1, 1)
    x_copy(slot_rows(-1, core), 4, 0, sibling)
    x_wait(slot_rows(1, core, 0), 2, 0)
    x_copy(slot_rows(1, core), 5, 0, sibling)
    def pairs(slot, own=False):
        row = st[slot]
        same = same_label(slot, own)
        value = ex[slot] * (own_a + row[0:1, :ROWS]) - jnp.where(same, own_c + row[1:2, :ROWS], 0.0)
        held = value.astype(BF16)
        pr[slot] = held
        return jnp.sum(held.astype(F32) * sc[slot], axis=1, keepdims=True)

    along = pairs(4, own=True)
    remote(st.at[0:8], st.at[0:8], st_send, st_recv, sibling).wait_recv()
    for slot in (0, 1, 2, 3, 5, 6, 7, 8):
        along = along + pairs(slot)
    along = along * (1.0 / SCALE)

    for step in (2, 1, 3, 0):
        x_to = wrap(x_me + step, NX)
        columns = pl.ds(pl.multiple_of(x_to * 256, 256), 256)
        total = jnp.dot(pr[0], win[0, :, columns], preferred_element_type=F32)
        for slot in range(1, SLOTS):
            total = total + jnp.dot(pr[slot], win[slot, :, columns], preferred_element_type=F32)
        grad = ((total - zn[:, columns] * along) * rnorm).astype(BF16)
        for which in (0, 1):
            gzs[x_to * 2 + which] = grad[:, which * SLICE : (which + 1) * SLICE]
        for which in (0, 1):
            if step == 0 and which == 0:
                target, device = x_me * 2 + 1 - core, sibling
            elif step == 0:
                continue
            else:
                target, device = x_to * 2 + which, x_peer(step, which)
            remote(gzs.at[target], gzg.at[own_rows, :], g_send, g_recv, device).start()
        if step == 2:
            for half in (0, 1):
                x_wait(slot_rows(2, core, half), 3, half)
            x_copy(slot_rows(2, core), 6, 0, sibling)
    gzg[own_rows, :] = gzs[own_x]

    x_wait(slot_rows(0, 1 - core), 0, 0)
    x_wait(slot_rows(-1, 1 - core), 4, 0)
    x_wait(slot_rows(1, 1 - core), 5, 0)
    x_wait(slot_rows(2, 1 - core), 6, 0)
    remote(gzs.at[0:7], gzs.at[0:7], g_send, g_recv, sibling).wait_recv()

    def y_self(yl, which):
        return jnp.logical_and(core == yh_me, jnp.logical_and(yl_me == yl, core == which))

    def y_copy(yl, which, part_no):
        rows = pl.ds(yl * (2 * YROWS) + which * YROWS + part_no * YPART, YPART)
        return remote(
            part.at[rows, :], yb.at[part_no, y_me], y_send, y_recv.at[part_no],
            ((yl * NZ + z_me) * 2 + which, x_me * NYH + core),
        )

    def y_start(yl, which, part_no):
        @pl.when(jnp.logical_not(y_self(yl, which)))
        def _():
            y_copy(yl, which, part_no).start()

        @pl.when(y_self(yl, which))
        def _():
            start = yl * (2 * YROWS) + which * YROWS + part_no * YPART
            yb[part_no, y_me] = part[start : start + YPART, :]

    grads = jnp.transpose(gzg[...])
    started = 0
    for n in range(E // 256):
        piece = jnp.dot(grads, embg[:, n * 256 : (n + 1) * 256], preferred_element_type=F32)
        part[n * 256 : (n + 1) * 256, :] = jnp.transpose(piece).astype(YTYPE)
        while (started + 1) * YROWS <= (n + 1) * 256:
            y_start(started // 2, started % 2, 0)
            started += 1
    for i in range(2 * NYL):
        y_start(i // 2, i % 2, 1)

    def z_copy(i, which):
        return remote(
            zs.at[i * 2 + which], zb.at[z_me], z_send, z_recv,
            ((yl_me * NZ + core * (NZ // 2) + i) * 2 + which, grp),
        )

    def z_self(i, which):
        return jnp.logical_and(z_me == core * (NZ // 2) + i, core == which)

    def y_wait(pieces, part_no):
        rows = yb.at[part_no, 0:pieces]
        remote(rows, rows, y_send, y_recv.at[part_no], sibling).wait_recv()

    for part_no in (0, 1):
        @pl.when(core == yh_me)
        def _(part_no=part_no):
            y_wait(NY - 1, part_no)

        @pl.when(core != yh_me)
        def _(part_no=part_no):
            y_wait(NY, part_no)

        total = yb[part_no, 0].astype(F32)
        for src in range(1, NY):
            total = total + yb[part_no, src].astype(F32)
        ysum[...] = total
        for i in range(part_no * (NZ // 4), (part_no + 1) * (NZ // 4)):
            for which in (0, 1):
                first = (i % (NZ // 4) * 2 + which) * ZROWS
                for row in range(ZROWS):
                    zs[i * 2 + which, row] = ysum[first + row : first + row + 1, :]

                @pl.when(jnp.logical_not(z_self(i, which)))
                def _(i=i, which=which):
                    z_copy(i, which).start()

                @pl.when(z_self(i, which))
                def _(i=i, which=which):
                    zb[z_me] = zs[i * 2 + which]

    @pl.when(core == z_core)
    def _():
        remote(zb.at[1:NZ], zb.at[1:NZ], z_send, z_recv, sibling).wait_recv()

    @pl.when(core != z_core)
    def _():
        remote(zb, zb, z_send, z_recv, sibling).wait_recv()

    total = zb[0]
    for src in range(1, NZ):
        total = total + zb[src]
    for row in range(ZROWS):
        head_ref[row : row + 1, :] = total[row]

    remote(win.at[0:8], win.at[0:8], halo_send, halo_whole.at[0], sibling).wait_send()
    remote(embg.at[0 : 7 * ROWS, :], embg.at[0 : 7 * ROWS, :], x_send, x_recv.at[0, 0], sibling).wait_send()
    remote(st.at[0:8], st.at[0:8], st_send, st_recv, sibling).wait_send()
    remote(gzs.at[0:7], gzs.at[0:7], g_send, g_recv, sibling).wait_send()

    @pl.when(core == yh_me)
    def _():
        remote(yb.at[:, 1:NY], yb.at[:, 1:NY], y_send, y_recv.at[0], sibling).wait_send()

    @pl.when(core != yh_me)
    def _():
        remote(yb, yb, y_send, y_recv.at[0], sibling).wait_send()

    @pl.when(core == z_core)
    def _():
        remote(zs.at[1:NZ], zs.at[1:NZ], z_send, z_recv, sibling).wait_send()

    @pl.when(core != z_core)
    def _():
        remote(zs, zs, z_send, z_recv, sibling).wait_send()


def hand_out(loss_in, head_in, loss_out, head_out, sem):
    first = pltpu.make_async_copy(loss_in, loss_out, sem.at[0])
    second = pltpu.make_async_copy(head_in, head_out, sem.at[1])
    first.start()
    second.start()
    first.wait()
    second.wait()


def on_device(embeddings, proj_weight, labels, flags):
    dma = pltpu.SemaphoreType.DMA
    loss, head = pl.pallas_call(
        kernel,
        out_shape=(pltpu.VMEM((ROWS,), F32), pltpu.VMEM((ZROWS, SLICE), F32)),
        in_specs=[pl.BlockSpec(memory_space=pl.ANY)] * 4,
        out_specs=(
            pl.BlockSpec(memory_space=pltpu.VMEM),
            pl.BlockSpec(memory_space=pltpu.VMEM),
        ),
        scratch_shapes=[
            pltpu.VMEM((E, WIDTH), BF16),
            pltpu.VMEM((SLOTS + 1, 16, 128), jnp.int32),
            pltpu.VMEM((16, 256), F32),
            pltpu.VMEM((2 * NX * ROWS, E), BF16),
            pltpu.VMEM((ROWS, WIDTH), F32),
            pltpu.VMEM((SLOTS, ROWS, WIDTH), BF16),
            pltpu.VMEM((SLOTS, ROWS, ROWS), F32),
            pltpu.VMEM((SLOTS, ROWS, ROWS), F32),
            pltpu.VMEM((SLOTS, ROWS, ROWS), BF16),
            pltpu.VMEM((SLOTS, 8, 256), F32),
            pltpu.VMEM((2 * NX, ROWS, SLICE), BF16),
            pltpu.VMEM((2 * NX * ROWS, SLICE), BF16),
            pltpu.VMEM((E, SLICE), YTYPE),
            pltpu.VMEM((2, NY, YPART, SLICE), YTYPE),
            pltpu.VMEM((YPART, SLICE), F32),
            pltpu.VMEM((NZ, ZROWS, 1, SLICE), F32),
            pltpu.VMEM((NZ, ZROWS, 1, SLICE), F32),
            dma((15,)),
            dma,
            dma((5, PIECES)),
            dma((SLOTS,)),
            dma,
            dma((7, 2)),
            dma,
            dma,
            dma,
            dma,
            dma,
            dma((2,)),
            dma,
            dma,
        ],
        compiler_params=pltpu.CompilerParams(
            collective_id=0, has_side_effects=True, vmem_limit_bytes=60 * 2**20
        ),
        name="contrastive_loss_and_head_gradient",
    )(embeddings, proj_weight, labels.reshape(LABEL_ROWS, 128), flags.reshape(LABEL_ROWS, 128))
    return pl.pallas_call(
        hand_out,
        out_shape=(
            jax.ShapeDtypeStruct((ROWS,), F32),
            jax.ShapeDtypeStruct((ZROWS, SLICE), F32),
        ),
        in_specs=[pl.BlockSpec(memory_space=pltpu.VMEM)] * 2,
        out_specs=(pl.BlockSpec(memory_space=pl.ANY), pl.BlockSpec(memory_space=pl.ANY)),
        scratch_shapes=[dma((2,))],
        compiler_params=pltpu.CompilerParams(vmem_limit_bytes=2**20),
        name="hand_out",
    )(loss, head)


def solution(mesh):
    return jax.shard_map(
        on_device,
        mesh=mesh,
        in_specs=(P(("blk", "grp"), None), P(), P(), P()),
        out_specs=(P(("blk", "grp")), P("blk", "grp")),
        check_vma=False,
    )
```

```python
import functools

import jax
import jax.numpy as jnp
from jax import lax
from jax.experimental import pallas as pl
from jax.experimental.pallas import tpu as pltpu
from jax.sharding import PartitionSpec as P

MESH = pl.DeviceIdType.MESH
F32 = jnp.float32
BF16 = jnp.bfloat16

NX, NYH, NYL, NZ = 4, 2, 4, 16
NY = NYH * NYL
ROWS, E, WIDTH = 192, 1280, 1024
SLOTS = 9
LABEL_ROWS = 1536
PIECES = 4
PIECE = ROWS // PIECES
HALFROWS = ROWS // 2
SLICE = 128
YROWS = E // NYL // 2
YPART = YROWS // 2
ZROWS = 10
SCALE = 10.0
YTYPE = BF16


def kernel(
    emb_hbm, w_hbm, lab_hbm, flag_hbm, loss_ref, head_ref,
    w_v, lab_v, lw, embg, zn, win, ex, sc, pr, st, gzs, gzg, part, yb, ysum, zs, zb,
    load_sem, halo_send, halo_recv, halo_whole, x_send, x_recv, st_send, st_recv,
    g_send, g_recv, y_send, y_recv, z_send, z_recv,
):
    blk = lax.axis_index("blk")
    grp = lax.axis_index("grp")
    blocks = 2 * NYL * NZ
    core = lax.rem(blk, 2)
    chip = blk // 2
    z_me = lax.rem(chip, NZ)
    yl_me = chip // NZ
    x_me = grp // NYH
    yh_me = lax.rem(grp, NYH)
    y_me = yh_me * NYL + yl_me
    own_x = x_me * 2 + core

    def wrap(value, size):
        return lax.rem(value + size, size)

    def chip_peer(step, which):
        return wrap(chip + step, blocks // 2) * 2 + which, grp

    def x_peer(step, which):
        return chip * 2 + which, wrap(x_me + step, NX) * NYH + yh_me

    sibling = (chip * 2 + 1 - core, grp)
    z_core = z_me // (NZ // 2)

    def remote(src, dst, send, recv, device):
        return pltpu.make_async_remote_copy(
            src_ref=src, dst_ref=dst, send_sem=send, recv_sem=recv, device_id=device, device_id_type=MESH
        )

    own_rows = pl.ds(pl.multiple_of(own_x * ROWS, 16), ROWS)
    loads = [pltpu.make_async_copy(emb_hbm, embg.at[own_rows, :], load_sem.at[0])]
    for n in range(4):
        columns = pl.ds(n * 256, 256)
        loads.append(pltpu.make_async_copy(w_hbm.at[:, columns], w_v.at[:, columns], load_sem.at[1 + n]))

    def label_start(block):
        row = block * 12 + (3 * grp) // 2
        first = jnp.minimum(row - lax.rem(row, 8), LABEL_ROWS - 16)
        return pl.multiple_of(first, 8), row - first

    for slot in range(SLOTS):
        rows = pl.ds(label_start(wrap(blk + slot - 4, blocks))[0], 16)
        loads.append(pltpu.make_async_copy(lab_hbm.at[rows, :], lab_v.at[slot], load_sem.at[5 + slot]))
    rows = pl.ds(label_start(blk)[0], 16)
    loads.append(pltpu.make_async_copy(flag_hbm.at[rows, :], lab_v.at[SLOTS], load_sem.at[5 + SLOTS]))
    for load in loads:
        load.start()

    barrier = pltpu.get_barrier_semaphore()

    def greet(device):
        pl.semaphore_signal(barrier, inc=1, device_id=device, device_id_type=MESH)

    for step in (1, -1, 2, -2, 3, -3, 4, -4):
        greet((wrap(blk + step, blocks), grp))
    for step in (1, 2, 3):
        for which in (0, 1):
            greet(x_peer(step, which))

    def greet_y(y_src, carry):
        @pl.when(jnp.logical_or(y_src != y_me, core != yh_me))
        def _():
            greet(((lax.rem(y_src, NYL) * NZ + z_me) * 2 + yh_me, x_me * NYH + y_src // NYL))
        return carry

    lax.fori_loop(0, NY, greet_y, 0)

    def greet_z(z_src, carry):
        @pl.when(jnp.logical_or(z_src != z_me, core != z_core))
        def _():
            greet(((yl_me * NZ + z_src) * 2 + z_core, grp))
        return carry

    lax.fori_loop(0, NZ, greet_z, 0)

    loads[0].wait()
    greeted = (
        8 + 6 + NY + NZ
        - jnp.where(core == yh_me, 1, 0).astype(jnp.int32)
        - jnp.where(core == z_core, 1, 0).astype(jnp.int32)
    )
    ahead, behind = chip_peer(1, core), chip_peer(-1, core)

    def halo_sem(slot, p):
        if isinstance(slot, int) and slot in (0, 2, 6, 8):
            return halo_recv.at[slot // 2, p]
        return halo_whole.at[slot]

    def halo(src_slot, dst_slot, p, device):
        rows = pl.ds(p * PIECE, PIECE)
        remote(
            win.at[src_slot, rows, :], win.at[dst_slot, rows, :],
            halo_send, halo_sem(dst_slot, p), device,
        ).start()

    def halo_wait(slot, p):
        rows = pl.ds(p * PIECE, PIECE)
        remote(win.at[slot, rows, :], win.at[slot, rows, :], halo_send, halo_sem(slot, p), sibling).wait_recv()

    def halo_wait_all(slot):
        remote(win.at[slot], win.at[slot], halo_send, halo_whole.at[slot], sibling).wait_recv()

    rnorms = []
    for half in (0, 1):
        rows = slice(half * HALFROWS, (half + 1) * HALFROWS)
        emb = embg[pl.ds(pl.multiple_of(own_x * ROWS + half * HALFROWS, 16), HALFROWS), :]
        ssq = jnp.zeros((HALFROWS, 1), F32)
        for n in range(4):
            columns = pl.ds(n * 256, 256)
            if half == 0:
                loads[1 + n].wait()
            zc = jnp.dot(emb, w_v[:, columns], preferred_element_type=F32)
            zn[rows, columns] = zc
            ssq = ssq + jnp.sum(zc * zc, axis=1, keepdims=True)
        rnorms.append(1.0 / jnp.sqrt(ssq + 1e-6))
        for n in range(4):
            columns = pl.ds(n * 256, 256)
            zc = zn[rows, columns] * rnorms[half]
            zn[rows, columns] = zc
            win[4, rows, columns] = zc.astype(BF16)
        if half == 0:
            pl.semaphore_wait(barrier, greeted)
        for p in range(half * (PIECES // 2), (half + 1) * (PIECES // 2)):
            halo(4, 2, p, ahead)
            halo(4, 6, p, behind)
            halo(4, 3 + 2 * core, p, sibling)
    rnorm = jnp.concatenate(rnorms, axis=0)

    right, left = x_peer(1, core), x_peer(-1, core)

    def slot_rows(x_step, which, half=None):
        start = (wrap(x_me + x_step, NX) * 2 + which) * ROWS
        if half is None:
            return pl.ds(pl.multiple_of(start, 16), ROWS)
        return pl.ds(pl.multiple_of(start + half * HALFROWS, 16), HALFROWS)

    def x_copy(rows, recv, half, device):
        remote(embg.at[rows, :], embg.at[rows, :], x_send, x_recv.at[recv, half], device).start()

    def x_wait(rows, recv, half):
        remote(embg.at[rows, :], embg.at[rows, :], x_send, x_recv.at[recv, half], sibling).wait_recv()

    for load in loads[5:]:
        load.wait()
    odd = lax.rem(grp, 2) == 1

    lw[...] = jnp.zeros_like(lw)
    for slot in range(SLOTS + 1):
        offset = label_start(wrap(blk + slot - 4, blocks) if slot < SLOTS else blk)[1]
        lw[slot : slot + 1, 0:128] = lab_v[slot, pl.ds(offset, 1), :].astype(F32)
        lw[slot : slot + 1, 128:256] = lab_v[slot, pl.ds(offset + 1, 1), :].astype(F32)
    plain = lw[...]
    lw[...] = jnp.where(odd, pltpu.roll(plain, 192, 1), plain)
    turned = jnp.transpose(jnp.concatenate([lw[...], jnp.zeros((112, 256), F32)], axis=0))
    own_lab = turned[:ROWS, 4:5]
    own_w = jnp.where(turned[:ROWS, SLOTS : SLOTS + 1] == 1.0, 0.5, 1.0)
    diagonal = lax.broadcasted_iota(jnp.int32, (ROWS, ROWS), 0) == lax.broadcasted_iota(
        jnp.int32, (ROWS, ROWS), 1
    )

    def same_label(slot, own):
        same = own_lab == lw[pl.ds(slot, 1), :ROWS]
        return jnp.logical_and(same, jnp.logical_not(diagonal)) if own else same

    own_unit = win[4]

    def scores(slot, sums, own=False):
        denom, possum, count = sums
        s = SCALE * lax.dot_general(
            own_unit, win[slot], (((1,), (1,)), ((), ())), preferred_element_type=F32
        )
        e = jnp.exp(s)
        if own:
            e = jnp.where(diagonal, 0.0, e)
        same = same_label(slot, own)
        ex[slot] = e
        sc[slot] = s
        denom = denom + jnp.sum(e, axis=1, keepdims=True)
        possum = possum + jnp.sum(jnp.where(same, s, 0.0), axis=1, keepdims=True)
        count = count + jnp.sum(jnp.where(same, 1.0, 0.0), axis=1, keepdims=True)
        return denom, possum, count

    nought = jnp.zeros((ROWS, 1), F32)
    sums = scores(4, (nought, nought, nought), own=True)

    for p in range(PIECES):
        halo_wait(2, p)
        halo(2, 0, p, ahead)
        halo(2, 1 + 2 * core, p, sibling)
        halo_wait(6, p)
        halo(6, 8, p, behind)
        halo(6, 5 + 2 * core, p, sibling)
        if p == 1:
            x_copy(own_rows, 0, 0, sibling)
            for half in (0, 1):
                x_copy(slot_rows(0, core, half), 1, half, right)
            for half in (1, 0):
                x_copy(slot_rows(0, core, half), 2, half, left)
    x_wait(slot_rows(-1, core, 0), 1, 0)
    x_copy(slot_rows(-1, core, 0), 3, 0, right)
    x_wait(slot_rows(1, core, 1), 2, 1)
    x_copy(slot_rows(1, core, 1), 3, 1, left)
    sums = scores(2, sums)
    sums = scores(6, sums)
    for slot in (5 - 2 * core, 3 - 2 * core, 7 - 2 * core):
        halo_wait_all(slot)
        sums = scores(slot, sums)

    @pl.when(core == 0)
    def _():
        for p in range(PIECES):
            halo_wait(8, p)
            halo(8, 7, p, sibling)
        for p in range(PIECES):
            halo_wait(0, p)

    @pl.when(core == 1)
    def _():
        for p in range(PIECES):
            halo_wait(0, p)
            halo(0, 1, p, sibling)
        for p in range(PIECES):
            halo_wait(8, p)

    sums = scores(0, sums)
    sums = scores(8, sums)
    halo_wait_all(1 + 6 * core)
    sums = scores(1 + 6 * core, sums)

    denom, possum, count = sums
    inv_count = 1.0 / jnp.maximum(count, 1.0)
    own_loss = own_w * (jnp.log(denom) - possum * inv_count)
    own_a = (SCALE * own_w) / denom
    own_c = (SCALE * own_w) * inv_count
    lane = lax.broadcasted_iota(jnp.int32, (ROWS, 128), 1)
    columns = jnp.where(lane == 0, own_a, jnp.where(lane == 1, own_c, own_loss))
    flat = jnp.transpose(jnp.concatenate([columns, jnp.zeros((64, 128), F32)], axis=0))
    st[4] = flat[:8]
    loss_ref[...] = flat[2, :ROWS]
    for step in (4, -4, 3, -3, 2, -2, 1, -1):
        remote(st.at[4], st.at[4 - step], st_send, st_recv, (wrap(blk + step, blocks), grp)).start()

    x_wait(slot_rows(-1, core, 1), 1, 1)
    x_copy(slot_rows(-1, core), 4, 0, sibling)
    x_wait(slot_rows(1, core, 0), 2, 0)
    x_copy(slot_rows(1, core), 5, 0, sibling)
    def pairs(slot, own=False):
        row = st[slot]
        same = same_label(slot, own)
        value = ex[slot] * (own_a + row[0:1, :ROWS]) - jnp.where(same, own_c + row[1:2, :ROWS], 0.0)
        held = value.astype(BF16)
        pr[slot] = held
        return jnp.sum(held.astype(F32) * sc[slot], axis=1, keepdims=True)

    along = pairs(4, own=True)
    remote(st.at[0:8], st.at[0:8], st_send, st_recv, sibling).wait_recv()
    for slot in (0, 1, 2, 3, 5, 6, 7, 8):
        along = along + pairs(slot)
    along = along * (1.0 / SCALE)

    for step in (2, 1, 3, 0):
        x_to = wrap(x_me + step, NX)
        columns = pl.ds(pl.multiple_of(x_to * 256, 256), 256)
        total = jnp.dot(pr[0], win[0, :, columns], preferred_element_type=F32)
        for slot in range(1, SLOTS):
            total = total + jnp.dot(pr[slot], win[slot, :, columns], preferred_element_type=F32)
        grad = ((total - zn[:, columns] * along) * rnorm).astype(BF16)
        for which in (0, 1):
            gzs[x_to * 2 + which] = grad[:, which * SLICE : (which + 1) * SLICE]
        for which in (0, 1):
            if step == 0 and which == 0:
                target, device = x_me * 2 + 1 - core, sibling
            elif step == 0:
                continue
            else:
                target, device = x_to * 2 + which, x_peer(step, which)
            remote(gzs.at[target], gzg.at[own_rows, :], g_send, g_recv, device).start()
        if step == 2:
            for half in (0, 1):
                x_wait(slot_rows(2, core, half), 3, half)
            x_copy(slot_rows(2, core), 6, 0, sibling)
    gzg[own_rows, :] = gzs[own_x]

    x_wait(slot_rows(0, 1 - core), 0, 0)
    x_wait(slot_rows(-1, 1 - core), 4, 0)
    x_wait(slot_rows(1, 1 - core), 5, 0)
    x_wait(slot_rows(2, 1 - core), 6, 0)
    remote(gzs.at[0:7], gzs.at[0:7], g_send, g_recv, sibling).wait_recv()

    def y_self(yl, which):
        return jnp.logical_and(core == yh_me, jnp.logical_and(yl_me == yl, core == which))

    def y_copy(yl, which, part_no):
        rows = pl.ds(yl * (2 * YROWS) + which * YROWS + part_no * YPART, YPART)
        return remote(
            part.at[rows, :], yb.at[part_no, y_me], y_send, y_recv.at[part_no],
            ((yl * NZ + z_me) * 2 + which, x_me * NYH + core),
        )

    def y_start(yl, which, part_no):
        @pl.when(jnp.logical_not(y_self(yl, which)))
        def _():
            y_copy(yl, which, part_no).start()

        @pl.when(y_self(yl, which))
        def _():
            start = yl * (2 * YROWS) + which * YROWS + part_no * YPART
            yb[part_no, y_me] = part[start : start + YPART, :]

    grads = jnp.transpose(gzg[...])
    started = 0
    for n in range(E // 256):
        piece = jnp.dot(grads, embg[:, n * 256 : (n + 1) * 256], preferred_element_type=F32)
        part[n * 256 : (n + 1) * 256, :] = jnp.transpose(piece).astype(YTYPE)
        while (started + 1) * YROWS <= (n + 1) * 256:
            y_start(started // 2, started % 2, 0)
            started += 1
    for i in range(2 * NYL):
        y_start(i // 2, i % 2, 1)

    def z_copy(i, which):
        return remote(
            zs.at[i * 2 + which], zb.at[z_me], z_send, z_recv,
            ((yl_me * NZ + core * (NZ // 2) + i) * 2 + which, grp),
        )

    def z_self(i, which):
        return jnp.logical_and(z_me == core * (NZ // 2) + i, core == which)

    def y_wait(pieces, part_no):
        rows = yb.at[part_no, 0:pieces]
        remote(rows, rows, y_send, y_recv.at[part_no], sibling).wait_recv()

    for part_no in (0, 1):
        @pl.when(core == yh_me)
        def _(part_no=part_no):
            y_wait(NY - 1, part_no)

        @pl.when(core != yh_me)
        def _(part_no=part_no):
            y_wait(NY, part_no)

        total = yb[part_no, 0].astype(F32)
        for src in range(1, NY):
            total = total + yb[part_no, src].astype(F32)
        ysum[...] = total
        for i in range(part_no * (NZ // 4), (part_no + 1) * (NZ // 4)):
            for which in (0, 1):
                first = (i % (NZ // 4) * 2 + which) * ZROWS
                for row in range(ZROWS):
                    zs[i * 2 + which, row] = ysum[first + row : first + row + 1, :]

                @pl.when(jnp.logical_not(z_self(i, which)))
                def _(i=i, which=which):
                    z_copy(i, which).start()

                @pl.when(z_self(i, which))
                def _(i=i, which=which):
                    zb[z_me] = zs[i * 2 + which]

    @pl.when(core == z_core)
    def _():
        remote(zb.at[1:NZ], zb.at[1:NZ], z_send, z_recv, sibling).wait_recv()

    @pl.when(core != z_core)
    def _():
        remote(zb, zb, z_send, z_recv, sibling).wait_recv()

    total = zb[0]
    for src in range(1, NZ):
        total = total + zb[src]
    for row in range(ZROWS):
        head_ref[row : row + 1, :] = total[row]

    remote(win.at[0:8], win.at[0:8], halo_send, halo_whole.at[0], sibling).wait_send()
    remote(embg.at[0 : 7 * ROWS, :], embg.at[0 : 7 * ROWS, :], x_send, x_recv.at[0, 0], sibling).wait_send()
    remote(st.at[0:8], st.at[0:8], st_send, st_recv, sibling).wait_send()
    remote(gzs.at[0:7], gzs.at[0:7], g_send, g_recv, sibling).wait_send()

    @pl.when(core == yh_me)
    def _():
        remote(yb.at[:, 1:NY], yb.at[:, 1:NY], y_send, y_recv.at[0], sibling).wait_send()

    @pl.when(core != yh_me)
    def _():
        remote(yb, yb, y_send, y_recv.at[0], sibling).wait_send()

    @pl.when(core == z_core)
    def _():
        remote(zs.at[1:NZ], zs.at[1:NZ], z_send, z_recv, sibling).wait_send()

    @pl.when(core != z_core)
    def _():
        remote(zs, zs, z_send, z_recv, sibling).wait_send()


def hand_out(loss_in, head_in, loss_out, head_out, sem):
    first = pltpu.make_async_copy(loss_in, loss_out, sem.at[0])
    second = pltpu.make_async_copy(head_in, head_out, sem.at[1])
    first.start()
    second.start()
    first.wait()
    second.wait()


def on_device(embeddings, proj_weight, labels, flags):
    dma = pltpu.SemaphoreType.DMA
    loss, head = pl.pallas_call(
        kernel,
        out_shape=(pltpu.VMEM((ROWS,), F32), pltpu.VMEM((ZROWS, SLICE), F32)),
        in_specs=[pl.BlockSpec(memory_space=pl.ANY)] * 4,
        out_specs=(
            pl.BlockSpec(memory_space=pltpu.VMEM),
            pl.BlockSpec(memory_space=pltpu.VMEM),
        ),
        scratch_shapes=[
            pltpu.VMEM((E, WIDTH), BF16),
            pltpu.VMEM((SLOTS + 1, 16, 128), jnp.int32),
            pltpu.VMEM((16, 256), F32),
            pltpu.VMEM((2 * NX * ROWS, E), BF16),
            pltpu.VMEM((ROWS, WIDTH), F32),
            pltpu.VMEM((SLOTS, ROWS, WIDTH), BF16),
            pltpu.VMEM((SLOTS, ROWS, ROWS), F32),
            pltpu.VMEM((SLOTS, ROWS, ROWS), F32),
            pltpu.VMEM((SLOTS, ROWS, ROWS), BF16),
            pltpu.VMEM((SLOTS, 8, 256), F32),
            pltpu.VMEM((2 * NX, ROWS, SLICE), BF16),
            pltpu.VMEM((2 * NX * ROWS, SLICE), BF16),
            pltpu.VMEM((E, SLICE), YTYPE),
            pltpu.VMEM((2, NY, YPART, SLICE), YTYPE),
            pltpu.VMEM((YPART, SLICE), F32),
            pltpu.VMEM((NZ, ZROWS, 1, SLICE), F32),
            pltpu.VMEM((NZ, ZROWS, 1, SLICE), F32),
            dma((15,)),
            dma,
            dma((5, PIECES)),
            dma((SLOTS,)),
            dma,
            dma((7, 2)),
            dma,
            dma,
            dma,
            dma,
            dma,
            dma((2,)),
            dma,
            dma,
        ],
        compiler_params=pltpu.CompilerParams(
            collective_id=0, has_side_effects=True, vmem_limit_bytes=60 * 2**20
        ),
        name="contrastive_loss_and_head_gradient",
    )(embeddings, proj_weight, labels.reshape(LABEL_ROWS, 128), flags.reshape(LABEL_ROWS, 128))
    return pl.pallas_call(
        hand_out,
        out_shape=(
            jax.ShapeDtypeStruct((ROWS,), F32),
            jax.ShapeDtypeStruct((ZROWS, SLICE), F32),
        ),
        in_specs=[pl.BlockSpec(memory_space=pltpu.VMEM)] * 2,
        out_specs=(pl.BlockSpec(memory_space=pl.ANY), pl.BlockSpec(memory_space=pl.ANY)),
        scratch_shapes=[dma((2,))],
        compiler_params=pltpu.CompilerParams(vmem_limit_bytes=2**20),
        name="hand_out",
    )(loss, head)


def solution(mesh):
    return jax.shard_map(
        on_device,
        mesh=mesh,
        in_specs=(P(("blk", "grp"), None), P(), P(), P()),
        out_specs=(P(("blk", "grp")), P("blk", "grp")),
        check_vma=False,
    )
```
